512 devices in a mesh: frame: 16 (over y_hi, x, core), expert: 32 (over y_lo, z).
Axes of the slice: x: 4, y: 8 (y_hi: 2, y_lo: 4; y = y_hi * 4 + y_lo), z: 8, core: 2. Of those that a mesh axis runs over, the one named last changes fastest.
Arguments:
- video: bfloat16 [32, 128, 64, 128], P('frame', 'expert'), may hold values from -6 to 6
- conv_weight: bfloat16 [3, 3, 3, 128, 128], replicated, may hold values from -0.109375 to 0.109375
- latent_weight: bfloat16 [128, 16], replicated, may hold values from -0.5 to 0.5
- embed_weight: bfloat16 [128, 1536], P(None, 'frame'), may hold values from -0.5 to 0.5
- context: bfloat16 [32768, 1536], P(('frame', 'expert')), may hold values from -6 to 6
- router_weight: bfloat16 [2, 1536, 32], P(None, None, 'expert'), may hold values from -0.15625 to 0.15625
- gate_weight: bfloat16 [32, 1536, 3072], P('expert', None, 'frame'), may hold values from -0.15625 to 0.15625
- up_weight: bfloat16 [32, 1536, 3072], P('expert', None, 'frame'), may hold values from -0.15625 to 0.15625
- down_weight: bfloat16 [32, 3072, 1536], P('expert', 'frame'), may hold values from -0.15625 to 0.15625
- routes: int32 [32768, 2], P(('frame', 'expert')), may hold values from 0 to 63, all different within a row
Outputs:
- moe_out: bfloat16 [32768, 1536], P(('frame', 'expert'))
The draws below stay inside these ranges and needn't reach their ends.
Inputs may be any that keep to these rules, and one draw needn't show every extreme that they name: `routes`: the two experts of a token differ.
All inputs are finite; a program needn't handle non-finite values.
Results may differ from the reference program's by a relative error of at most 0.024.
Values may be sent and summed in bfloat16 or wider, within the bound.
No kernel may reach another device: no remote copies, remote signals or barrier semaphores. Data moves between devices by JAX's collectives and lax.ppermute only.
A program may use at most 64 MiB of HBM per device.

```python
import jax
import jax.numpy as jnp
from jax import lax

C = 128
LAT = 16
D = 1536
FF = 1536
COLS = 64
TOK_DEV = 64
FRAMES = 32
HEIGHT = 128
TOKENS = 32768
EXPERTS = 64
PATCH = 128
CAP = 2
N_FRAME = 16
N_EXPERT = 32


def block_scale(stream_key, extent, shards, least, top_value):
    loudness, own = 1.0, jax.random.fold_in(stream_key, 6)
    for axis_at, blocks in shards:
        heights = jnp.exp(jax.random.uniform(jax.random.fold_in(own, axis_at), (blocks,), jnp.float32, least / len(shards), top_value / len(shards)))
        loudness = loudness * jnp.repeat(heights, extent[axis_at] // blocks).reshape([-1 if axis == axis_at else 1 for axis in range(len(extent))])
    return loudness


def different_ones(own_key, rows, amount, top, lift):
    ranking = jax.random.permutation(jax.random.fold_in(own_key, 1), amount)
    favour = ranking
    for power in range(3):
        favour = favour * favour // amount
    favour = favour * lift // amount
    lots = jax.random.randint(jax.random.fold_in(own_key, 2), (rows, amount), 0, 4096) + favour
    fixed_rows = jax.random.permutation(jax.random.fold_in(own_key, 3), rows)[jnp.arange(amount) % rows]
    lots = jnp.where(jnp.arange(rows)[:, None] == fixed_rows[None, :], 1 << 14, lots)
    score = lots * amount + jnp.arange(amount)
    return lax.top_k(score.astype(jnp.int32), top)[1].astype(jnp.int32)


def normal_values(rng, dims, spread, most, pieces=(), kind=jnp.bfloat16):
    loudness = block_scale(rng, dims, pieces, -0.22, 0.18) if pieces else 1.0
    array = jax.random.normal(rng, dims, jnp.float32) * spread * loudness
    return jnp.minimum(jnp.maximum(array, -most), most).astype(kind)


def setup_inputs(seed: int = 0) -> dict:
    key_list = jax.random.split(jax.random.key(seed), 11)
    return {
        "video": normal_values(key_list[0], (FRAMES, HEIGHT, COLS, C), 1.0, 6.0, ((0, 16), (1, 32))),
        "conv_weight": normal_values(key_list[1], (3, 3, 3, C, C), (27 * C) ** -0.5, 0.109375),
        "latent_weight": normal_values(key_list[2], (C, LAT), C ** -0.5, 0.5),
        "embed_weight": normal_values(key_list[3], (PATCH, D), PATCH ** -0.5, 0.5, ((1, 16),)),
        "context": normal_values(key_list[4], (TOKENS, D), 1.0, 6.0, ((0, 512),)),
        "router_weight": normal_values(key_list[5], (2, D, N_EXPERT), D ** -0.5, 0.15625, ((2, 32),)),
        "gate_weight": normal_values(key_list[6], (N_EXPERT, D, 2 * FF), D ** -0.5, 0.15625, ((0, 32), (2, 16))),
        "up_weight": normal_values(key_list[7], (N_EXPERT, D, 2 * FF), D ** -0.5, 0.15625, ((0, 32), (2, 16))),
        "down_weight": normal_values(key_list[8], (N_EXPERT, 2 * FF, D), FF ** -0.5, 0.15625, ((0, 32), (1, 16))),
        "routes": different_ones(key_list[9], TOKENS, EXPERTS, 2, 512),
    }


def encode(video, conv_weight, latent_weight, embed_weight, context):
    padded = jnp.pad(video, ((2, 0), (1, 1), (1, 1), (0, 0)))
    total = jnp.zeros((FRAMES * HEIGHT * COLS, C), jnp.float32)
    for a in range(3):
        for b in range(3):
            for q in range(3):
                window = padded[a:a + FRAMES, b:b + HEIGHT, q:q + COLS, :].reshape(-1, C)
                total = total + jnp.dot(window, conv_weight[a, b, q], preferred_element_type=jnp.float32)
    feature = (video.reshape(-1, C).astype(jnp.float32) + jax.nn.silu(total)).astype(jnp.bfloat16)
    latent = jnp.dot(feature, latent_weight, preferred_element_type=jnp.float32).astype(jnp.bfloat16)
    blocks = latent.reshape(FRAMES // 2, 2, HEIGHT // 2, 2, COLS // 2, 2, LAT)
    patches = blocks.transpose(0, 2, 4, 1, 3, 5, 6).reshape(TOKENS, PATCH)
    embedded = jnp.dot(patches, embed_weight, preferred_element_type=jnp.float32).astype(jnp.bfloat16)
    summed = embedded.astype(jnp.float32) + context.astype(jnp.float32)
    meansq = lax.optimization_barrier(jnp.mean(summed * summed, axis=1, keepdims=True))
    return (summed * lax.rsqrt(meansq + 1e-06)).astype(jnp.bfloat16)

def reference(video, conv_weight, latent_weight, embed_weight, context, router_weight, gate_weight, up_weight, down_weight, routes):
    tokens = encode(video, conv_weight, latent_weight, embed_weight, context)
    flat_routes = routes.reshape(-1).astype(jnp.int32)
    assigned = flat_routes.shape[0]
    sources = N_FRAME * N_EXPERT
    labels = jnp.arange(EXPERTS, dtype=jnp.int32)
    chosen = (flat_routes.reshape(sources, 2 * TOK_DEV)[:, :, None] == labels[None, None, :]).astype(jnp.int32)
    earlier = jnp.cumsum(chosen, axis=1) - chosen
    rank = lax.optimization_barrier(jnp.sum(earlier * chosen, axis=2)).reshape(-1).astype(jnp.int32)
    keep = rank < CAP
    limit = sources * CAP
    position = jnp.arange(assigned, dtype=jnp.int32)
    source = position // (2 * TOK_DEV)
    slot = jnp.where(keep, flat_routes * limit + source * CAP + rank, EXPERTS * limit).astype(jnp.int32)
    holder = jnp.zeros((EXPERTS * limit + 1,), jnp.int32).at[slot].set(position // 2)
    holder = holder[:EXPERTS * limit].reshape(EXPERTS, limit)
    groups = N_FRAME // 2
    group_width = FF // groups

    def one_expert(expert):
        half = expert // N_EXPERT
        owner = expert % N_EXPERT
        index = lax.dynamic_index_in_dim(holder, expert, 0, keepdims=False)
        rows_in = tokens[index]
        router_pair = lax.dynamic_index_in_dim(router_weight, half, 0, keepdims=False)
        router_column = lax.dynamic_index_in_dim(router_pair, owner, 1, keepdims=False)
        gate_all = lax.dynamic_index_in_dim(gate_weight, owner, 0, keepdims=False)
        up_all = lax.dynamic_index_in_dim(up_weight, owner, 0, keepdims=False)
        down_all = lax.dynamic_index_in_dim(down_weight, owner, 0, keepdims=False)
        w_gate = lax.dynamic_slice_in_dim(gate_all, half * FF, FF, 1)
        w_up = lax.dynamic_slice_in_dim(up_all, half * FF, FF, 1)
        w_down = lax.dynamic_slice_in_dim(down_all, half * FF, FF, 0)
        score = jax.nn.sigmoid(jnp.dot(rows_in, router_column[:, None], preferred_element_type=jnp.float32))
        gate = jnp.dot(rows_in, w_gate, preferred_element_type=jnp.float32)
        up = jnp.dot(rows_in, w_up, preferred_element_type=jnp.float32)
        hidden = (jax.nn.silu(gate) * up).astype(jnp.bfloat16)
        summed = jnp.zeros((limit, D), jnp.float32)
        for group in range(groups):
            lower = group * group_width
            product = jnp.dot(hidden[:, lower:lower + group_width], w_down[lower:lower + group_width], preferred_element_type=jnp.float32)
            partial_value = lax.optimization_barrier((score * product).astype(jnp.bfloat16))
            summed = summed + partial_value.astype(jnp.float32)
        return summed.astype(jnp.bfloat16)
    results = lax.map(one_expert, labels).reshape(EXPERTS * limit, D)
    safe_slot = jnp.where(keep, slot, 0).astype(jnp.int32)
    picked = jnp.where(keep[:, None], results[safe_slot].astype(jnp.float32), jnp.zeros((), jnp.float32))
    return lax.optimization_barrier(jnp.sum(picked.reshape(TOKENS, 2, D), axis=1)).astype(jnp.bfloat16)
```

```python
import jax
import jax.numpy as jnp
from jax import lax
from jax.sharding import Mesh, PartitionSpec as P

FRAME = ("yh", "x", "c")
EXPERT = ("yl", "z")
SOURCES = ("yh", "yl", "z")
SIZES = (2, 4, 2, 4, 8)
NAMES = ("yh", "x", "c", "yl", "z")
BF = jnp.bfloat16
F32 = jnp.float32


def dot(a, b, dims=((1,), (0,))):
    return lax.dot_general(a, b, (dims, ((), ())), preferred_element_type=F32)


def shifted(value, axes, step):
    count = lax.axis_size(axes)
    pairs = [(i, i + step) for i in range(count) if 0 <= i + step < count]
    return lax.ppermute(value, axes, pairs)


def encode(video, conv_weight, latent_weight):
    frames, rows, cols, chans = video.shape
    above = shifted(video[:, rows - 1 :], EXPERT, 1)
    below = shifted(video[:, :1], EXPERT, -1)
    tall = jnp.concatenate([above, video, below], axis=1)
    past = shifted(tall, FRAME, 1)

    def windows(block):
        wide = jnp.pad(block, ((0, 0), (0, 0), (1, 1), (0, 0)))
        taps = [wide[:, b : b + rows, q : q + cols] for b in range(3) for q in range(3)]
        return jnp.concatenate(taps, axis=-1).reshape(block.shape[0], rows * cols, 9 * chans)

    kernel = conv_weight.reshape(3, 9 * chans, chans)
    own, old = windows(tall), windows(past)
    first = dot(own[0], kernel[2]) + dot(old[0], kernel[0]) + dot(old[1], kernel[1])
    second = dot(own[1], kernel[2]) + dot(own[0], kernel[1]) + dot(old[1], kernel[0])
    mixed = jnp.concatenate([first, second], axis=0)
    feature = (video.reshape(-1, chans).astype(F32) + jax.nn.silu(mixed)).astype(BF)
    return dot(feature, latent_weight).astype(BF)


def place_table(routes, experts, capacity):
    tok = routes.shape[0]
    flat = routes.reshape(-1)
    count = flat.shape[0]
    chosen = (flat[:, None] == jnp.arange(experts, dtype=jnp.int32)[None, :]).astype(BF)
    at = jnp.arange(count, dtype=jnp.int32)
    before = (at[:, None] > at[None, :]).astype(BF)
    rank = jnp.sum(dot(before, chosen) * chosen.astype(F32), axis=1).astype(jnp.int32)
    place = jnp.where(rank < capacity, flat * capacity + rank, -1).reshape(tok, 2)
    slots = jnp.arange(experts * capacity, dtype=jnp.int32)[None, :]
    hit = (place[:, :1] == slots) | (place[:, 1:] == slots)
    return hit.astype(BF)


def local(
    video,
    conv_weight,
    latent_weight,
    embed_weight,
    context,
    router_weight,
    gate_weight,
    up_weight,
    down_weight,
    routes,
):
    rows, cols = video.shape[1:3]
    tok, width = context.shape
    experts, capacity = 64, 2
    share = down_weight.shape[1]

    held = jnp.concatenate([gate_weight[0].T, up_weight[0].T, down_weight[0]], axis=0)
    held = lax.all_gather(held, "x", axis=0, tiled=False)

    part = embed_weight.T
    spread = lax.all_gather(jnp.concatenate([part] * 3, axis=0), FRAME, axis=0, tiled=False)
    embed = spread[:, : part.shape[0]].reshape(width, part.shape[1])

    table = place_table(routes, experts, capacity)
    latent = encode(video, conv_weight, latent_weight)
    lat = latent.shape[1]
    blocks = latent.reshape(2, rows // 2, 2, cols // 2, 2, lat)
    patches = blocks.transpose(1, 3, 0, 2, 4, 5).reshape(tok, 8 * lat)
    embedded = dot(patches, embed, ((1,), (1,))).astype(BF)
    total = embedded.astype(F32) + context.astype(F32)
    meansq = jnp.mean(total * total, axis=1, keepdims=True)
    tokens = (total * lax.rsqrt(meansq + 1e-06)).astype(BF)

    outgoing = dot(table, tokens, ((0,), (0,))).astype(BF).reshape(experts, capacity, width)
    arrived = lax.all_to_all(outgoing, SOURCES, split_axis=0, concat_axis=0, tiled=True)
    mine = arrived.reshape(experts * capacity, width)
    swap = [(0, 1), (1, 0)]
    theirs = lax.ppermute(mine, "c", swap)
    inputs = jnp.concatenate([theirs, mine], axis=0)
    router = lax.dynamic_index_in_dim(router_weight, lax.axis_index("yh"), 0, keepdims=False)
    score = jax.nn.sigmoid(dot(inputs, router))
    result = jnp.zeros((2 * experts * capacity, width), F32)
    for chunk in range(held.shape[0]):
        gate = dot(inputs, held[chunk, :share], ((1,), (1,)))
        up = dot(inputs, held[chunk, share : 2 * share], ((1,), (1,)))
        hidden = (jax.nn.silu(gate) * up).astype(BF)
        result = result + dot(hidden, held[chunk, 2 * share :])
    result = (score * result).astype(BF)
    other, own = result[: experts * capacity], result[experts * capacity :]
    back = lax.ppermute(other, "c", swap)
    summed = (back.astype(F32) + own.astype(F32)).astype(BF).reshape(experts, capacity, width)
    homeward = lax.all_to_all(summed, SOURCES, split_axis=0, concat_axis=0, tiled=True)
    return dot(table, homeward.reshape(experts * capacity, width)).astype(BF)


def solution(mesh):
    fine = Mesh(mesh.devices.reshape(SIZES), NAMES)
    return jax.shard_map(
        local,
        mesh=fine,
        in_specs=(
            P(FRAME, EXPERT, None, None),
            P(),
            P(),
            P(None, FRAME),
            P((*FRAME, *EXPERT), None),
            P(None, None, EXPERT),
            P(EXPERT, None, FRAME),
            P(EXPERT, None, FRAME),
            P(EXPERT, FRAME, None),
            P((*FRAME, *EXPERT), None),
        ),
        out_specs=P((*FRAME, *EXPERT), None),
        check_vma=False,
    )
```

```python
import functools

import jax
import jax.numpy as jnp
from jax import lax
from jax.experimental import pallas as pl
from jax.experimental.pallas import tpu as pltpu
from jax.sharding import Mesh, PartitionSpec as P

FRAME = ("yh", "x", "c")
EXPERT = ("yl", "z")
SOURCES = ("yh", "yl", "z")
SIZES = (2, 4, 2, 4, 8)
NAMES = ("yh", "x", "c", "yl", "z")
BF = jnp.bfloat16
F32 = jnp.float32
SWAP = [(0, 1), (1, 0)]
VMEM_BYTES = 40 * 1024 * 1024


def dot(a, b, dims=((1,), (0,))):
    return lax.dot_general(a, b, (dims, ((), ())), preferred_element_type=F32)


def shifted(value, axes, step):
    count = lax.axis_size(axes)
    pairs = [(i, i + step) for i in range(count) if 0 <= i + step < count]
    return lax.ppermute(value, axes, pairs)


def ring(value, step):
    return lax.ppermute(value, "x", [(i, (i - step) % 4) for i in range(4)])


def encode(video, conv_weight, latent_weight):
    frames, rows, cols, chans = video.shape
    above = shifted(video[:, rows - 1 :], EXPERT, 1)
    below = shifted(video[:, :1], EXPERT, -1)
    tall = jnp.concatenate([above, video, below], axis=1)
    past = shifted(tall, FRAME, 1)

    def windows(block):
        wide = jnp.pad(block, ((0, 0), (0, 0), (1, 1), (0, 0)))
        taps = [wide[:, b : b + rows, q : q + cols] for b in range(3) for q in range(3)]
        return jnp.concatenate(taps, axis=-1).reshape(block.shape[0], rows * cols, 9 * chans)

    kernel = conv_weight.reshape(3, 9 * chans, chans)
    own, old = windows(tall), windows(past)
    first = dot(own[0], kernel[2]) + dot(old[0], kernel[0]) + dot(old[1], kernel[1])
    second = dot(own[1], kernel[2]) + dot(own[0], kernel[1]) + dot(old[1], kernel[0])
    mixed = jnp.concatenate([first, second], axis=0)
    feature = (video.reshape(-1, chans).astype(F32) + jax.nn.silu(mixed)).astype(BF)
    return dot(feature, latent_weight).astype(BF)


def place_table(routes, experts, capacity):
    tok = routes.shape[0]
    flat = routes.reshape(-1)
    count = flat.shape[0]
    chosen = (flat[:, None] == jnp.arange(experts, dtype=jnp.int32)[None, :]).astype(BF)
    at = jnp.arange(count, dtype=jnp.int32)
    before = (at[:, None] > at[None, :]).astype(BF)
    rank = jnp.sum(dot(before, chosen) * chosen.astype(F32), axis=1).astype(jnp.int32)
    place = jnp.where(rank < capacity, flat * capacity + rank, -1).reshape(tok, 2)
    slots = jnp.arange(experts * capacity, dtype=jnp.int32)[None, :]
    hit = (place[:, :1] == slots) | (place[:, 1:] == slots)
    return hit.astype(BF)


def dispatch_kernel(at_ref, own_ref, other_ref, patches_ref, context_ref, table_ref, out_ref, embed_ref):
    yh, x, c = at_ref[0], at_ref[1], at_ref[2]
    for shard in range(16):
        away = jnp.abs(shard // 8 - yh)
        turn = lax.rem(shard // 2 % 4 - x + 4, 4)
        near = own_ref[away, turn]
        far = other_ref[away, turn]
        embed_ref[shard] = jnp.where(shard % 2 == c, near, far)
    width = context_ref.shape[1]
    embed = embed_ref[...].reshape(width, embed_ref.shape[2])
    embedded = dot(patches_ref[...], embed, ((1,), (1,))).astype(BF)
    total = embedded.astype(F32) + context_ref[...].astype(F32)
    meansq = jnp.mean(total * total, axis=1, keepdims=True)
    tokens = (total * lax.rsqrt(meansq + 1e-06)).astype(BF)
    out_ref[...] = dot(table_ref[...], tokens, ((0,), (0,))).astype(BF)


def expert_kernel(at_ref, inputs_ref, score_ref, held_ref, d0_ref, d1_ref, d2_ref, d3_ref, other_ref, own_ref, hidden_ref):
    step = pl.program_id(0)
    share = d0_ref.shape[0]
    both = dot(held_ref[0], inputs_ref[...])
    gate, up = both[:share], both[share:]
    hidden_ref[step] = (gate / (1.0 + jnp.exp(-gate)) * up).astype(BF).T

    @pl.when(step == pl.num_programs(0) - 1)
    def _():
        rows, width = other_ref.shape
        tile = 512
        score = score_ref[...]
        for at in range(0, width, tile):
            part = slice(at, at + tile)
            total = dot(hidden_ref[0], d0_ref[:, part])
            total += dot(hidden_ref[1], d1_ref[:, part])
            total += dot(hidden_ref[2], d2_ref[:, part])
            total += dot(hidden_ref[3], d3_ref[:, part])
            total = (total * score).astype(BF)
            other_ref[:, part] = total[:rows]
            own_ref[:, part] = total[rows:]


def local(
    video,
    conv_weight,
    latent_weight,
    embed_weight,
    context,
    router_weight,
    gate_weight,
    up_weight,
    down_weight,
    routes,
):
    rows, cols = video.shape[1:3]
    tok, width = context.shape
    experts, capacity = 64, 2
    slots = experts * capacity
    share = down_weight.shape[1]
    yh, x, c = lax.axis_index("yh"), lax.axis_index("x"), lax.axis_index("c")

    held = jnp.concatenate([gate_weight[0].T, up_weight[0].T], axis=0)
    held = lax.all_gather(held, "x", axis=0, tiled=False)

    part = embed_weight.T
    around = jnp.stack([part, ring(part, 1), ring(part, 2), ring(part, 3)])
    near = jnp.stack([around, lax.ppermute(around, "yh", SWAP)])
    far = lax.ppermute(near, "c", SWAP)

    d0 = down_weight[0]
    behind, ahead = ring(d0, -1), ring(d0, 1)
    opposite = jnp.concatenate([ring(behind[: share // 2], -1), ring(ahead[share // 2 :], 1)], axis=0)

    table = place_table(routes, experts, capacity)
    latent = encode(video, conv_weight, latent_weight)
    lat = latent.shape[1]
    blocks = latent.reshape(2, rows // 2, 2, cols // 2, 2, lat)
    patches = blocks.transpose(1, 3, 0, 2, 4, 5).reshape(tok, 8 * lat)

    vmem = pl.BlockSpec(memory_space=pltpu.VMEM)
    outgoing = pl.pallas_call(
        dispatch_kernel,
        out_shape=jax.ShapeDtypeStruct((slots, width), BF),
        in_specs=[pl.BlockSpec(memory_space=pltpu.SMEM)] + [vmem] * 5,
        out_specs=vmem,
        scratch_shapes=[pltpu.VMEM((16, *part.shape), BF)],
        compiler_params=pltpu.CompilerParams(vmem_limit_bytes=VMEM_BYTES),
    )(jnp.stack([yh, x, c]).astype(jnp.int32), near, far, patches, context, table)

    arrived = lax.all_to_all(outgoing.reshape(experts, capacity, width), SOURCES, split_axis=0, concat_axis=0, tiled=True)
    mine = arrived.reshape(slots, width)
    theirs = lax.ppermute(mine, "c", SWAP)
    inputs = jnp.concatenate([theirs, mine], axis=0)
    router = lax.dynamic_index_in_dim(router_weight, yh, 0, keepdims=False)
    score = jax.nn.sigmoid(dot(inputs, router))

    order = jnp.stack([x, x + 3, x + 2, x + 1]).astype(jnp.int32) % 4
    down = pl.BlockSpec((share, width), lambda i, at: (0, 0))
    half = pl.BlockSpec((slots, width), lambda i, at: (0, 0))
    other, own = pl.pallas_call(
        expert_kernel,
        out_shape=[jax.ShapeDtypeStruct((slots, width), BF)] * 2,
        grid_spec=pltpu.PrefetchScalarGridSpec(
            num_scalar_prefetch=1,
            grid=(4,),
            in_specs=[
                pl.BlockSpec((width, 2 * slots), lambda i, at: (0, 0)),
                pl.BlockSpec((2 * slots, 1), lambda i, at: (0, 0)),
                pl.BlockSpec((1, 2 * share, width), lambda i, at: (at[i], 0, 0)),
                down,
                down,
                down,
                down,
            ],
            out_specs=[half, half],
            scratch_shapes=[pltpu.VMEM((4, 2 * slots, share), BF)],
        ),
        compiler_params=pltpu.CompilerParams(vmem_limit_bytes=VMEM_BYTES),
    )(order, inputs.T, score, held, d0, behind, opposite, ahead)

    back = lax.ppermute(other, "c", SWAP)
    summed = (back.astype(F32) + own.astype(F32)).astype(BF).reshape(experts, capacity, width)
    homeward = lax.all_to_all(summed, SOURCES, split_axis=0, concat_axis=0, tiled=True)
    return dot(table, homeward.reshape(slots, width)).astype(BF)


def solution(mesh):
    fine = Mesh(mesh.devices.reshape(SIZES), NAMES)
    return jax.shard_map(
        local,
        mesh=fine,
        in_specs=(
            P(FRAME, EXPERT, None, None),
            P(),
            P(),
            P(None, FRAME),
            P((*FRAME, *EXPERT), None),
            P(None, None, EXPERT),
            P(EXPERT, None, FRAME),
            P(EXPERT, None, FRAME),
            P(EXPERT, FRAME, None),
            P((*FRAME, *EXPERT), None),
        ),
        out_specs=P((*FRAME, *EXPERT), None),
        check_vma=False,
    )
```

```python
import jax
import jax.numpy as jnp
from jax import lax
from jax.experimental import pallas as pl
from jax.experimental.pallas import tpu as pltpu
from jax.sharding import Mesh, PartitionSpec as P

FRAME = ("yh", "x", "c")
EXPERT = ("yl", "z")
SOURCES = ("yh", "yl", "z")
SIZES = (2, 4, 2, 4, 8)
NAMES = ("yh", "x", "c", "yl", "z")
BF = jnp.bfloat16
F32 = jnp.float32
SWAP = [(0, 1), (1, 0)]
XOR1 = [(i, i ^ 1) for i in range(4)]
XOR2 = [(i, i ^ 2) for i in range(4)]
VMEM_BYTES = 40 * 1024 * 1024


def dot(a, b, dims=((1,), (0,))):
    return lax.dot_general(a, b, (dims, ((), ())), preferred_element_type=F32)


def shifted(value, axes, step):
    count = lax.axis_size(axes)
    pairs = [(i, i + step) for i in range(count) if 0 <= i + step < count]
    return lax.ppermute(value, axes, pairs)


def ring(value, step):
    return lax.ppermute(value, "x", [(i, (i - step) % 4) for i in range(4)])


def encode(video, conv_weight, latent_weight):
    frames, rows, cols, chans = video.shape
    above = shifted(video[:, rows - 1 :], EXPERT, 1)
    below = shifted(video[:, :1], EXPERT, -1)
    tall = jnp.concatenate([above, video, below], axis=1)
    past = shifted(tall, FRAME, 1)

    def windows(block):
        wide = jnp.pad(block, ((0, 0), (0, 0), (1, 1), (0, 0)))
        taps = [wide[:, b : b + rows, q : q + cols] for b in range(3) for q in range(3)]
        return jnp.concatenate(taps, axis=-1).reshape(block.shape[0], rows * cols, 9 * chans)

    kernel = conv_weight.reshape(3, 9 * chans, chans)
    own, old = windows(tall), windows(past)
    first = dot(own[0], kernel[2]) + dot(old[0], kernel[0]) + dot(old[1], kernel[1])
    second = dot(own[1], kernel[2]) + dot(own[0], kernel[1]) + dot(old[1], kernel[0])
    mixed = jnp.concatenate([first, second], axis=0)
    feature = (video.reshape(-1, chans).astype(F32) + jax.nn.silu(mixed)).astype(BF)
    return dot(feature, latent_weight).astype(BF)


def place_table(routes, experts, capacity):
    tok = routes.shape[0]
    flat = routes.reshape(-1)
    count = flat.shape[0]
    chosen = (flat[:, None] == jnp.arange(experts, dtype=jnp.int32)[None, :]).astype(BF)
    at = jnp.arange(count, dtype=jnp.int32)
    before = (at[:, None] > at[None, :]).astype(BF)
    rank = jnp.sum(dot(before, chosen) * chosen.astype(F32), axis=1).astype(jnp.int32)
    place = jnp.where(rank < capacity, flat * capacity + rank, -1).reshape(tok, 2)
    slots = jnp.arange(experts * capacity, dtype=jnp.int32)[None, :]
    hit = (place[:, :1] == slots) | (place[:, 1:] == slots)
    return hit.astype(BF)


def dispatch_kernel(at_ref, near_ref, far_ref, patches_ref, context_ref, table_ref, out_ref, embed_ref):
    me = at_ref[0]
    for shard in range(16):
        apart = shard ^ me
        near, far = near_ref[apart // 2], far_ref[apart // 2]
        embed_ref[shard] = jnp.where(apart % 2 == 0, near, far)
    width = context_ref.shape[1]
    embed = embed_ref[...].reshape(width, embed_ref.shape[2])
    embedded = dot(patches_ref[...], embed, ((1,), (1,))).astype(BF)
    total = embedded.astype(F32) + context_ref[...].astype(F32)
    meansq = jnp.mean(total * total, axis=1, keepdims=True)
    tokens = (total * lax.rsqrt(meansq + 1e-06)).astype(BF)
    out_ref[...] = dot(table_ref[...], tokens, ((0,), (0,))).astype(BF)


def turn_kernel(mine_ref, theirs_ref, router_ref, out_ref, score_ref):
    rows = mine_ref.shape[0]
    for half, ref in enumerate((theirs_ref, mine_ref)):
        block = ref[...]
        at = slice(half * rows, (half + 1) * rows)
        out_ref[:, at] = block.T
        logit = jnp.sum(block.astype(F32) * router_ref[...].astype(F32), axis=1, keepdims=True)
        score_ref[at] = 1.0 / (1.0 + jnp.exp(-logit))


def expert_kernel(inputs_ref, score_ref, gate_ref, up_ref, down_ref, *refs):
    firsts, seconds = refs[0:3], refs[3:6]
    other_ref, own_ref, hidden_ref, held_ref = refs[6:]
    share, width = down_ref.shape
    inputs = inputs_ref[...]
    for chunk in range(4):
        gate = gate_ref[...] if chunk == 0 else firsts[chunk - 1][:share]
        up = up_ref[...] if chunk == 0 else seconds[chunk - 1][:share]
        gate, up = dot(gate, inputs), dot(up, inputs)
        at = chunk * share
        hidden_ref[:, at : at + share] = (gate / (1.0 + jnp.exp(-gate)) * up).T.astype(BF)
        if chunk == 0:
            held_ref[at : at + share] = down_ref[...]
        else:
            held_ref[at : at + share // 2] = firsts[chunk - 1][share:]
            held_ref[at + share // 2 : at + share] = seconds[chunk - 1][share:]
    rows, tile = other_ref.shape[0], 512
    for at in range(0, width, tile):
        part = slice(at, at + tile)
        total = dot(hidden_ref[...], held_ref[:, part])
        total = (total * score_ref[...]).astype(BF)
        other_ref[:, part] = total[:rows]
        own_ref[:, part] = total[rows:]


def local(
    video,
    conv_weight,
    latent_weight,
    embed_weight,
    context,
    router_weight,
    gate_weight,
    up_weight,
    down_weight,
    routes,
):
    rows, cols = video.shape[1:3]
    tok, width = context.shape
    experts, capacity = 64, 2
    slots = experts * capacity
    share = down_weight.shape[1]

    gate, up, down = gate_weight[0].T, up_weight[0].T, down_weight[0]
    first = jnp.concatenate([gate, down[: share // 2]], axis=0)
    second = jnp.concatenate([up, down[share // 2 :]], axis=0)
    first_behind, second_ahead = ring(first, -1), ring(second, 1)

    near = embed_weight.T[None]
    for axis, pairs in (("x", XOR1), ("x", XOR2), ("yh", SWAP)):
        near = jnp.concatenate([near, lax.ppermute(near, axis, pairs)], axis=0)
    far = lax.ppermute(near, "c", SWAP)

    table = place_table(routes, experts, capacity)
    latent = encode(video, conv_weight, latent_weight)
    lat = latent.shape[1]
    blocks = latent.reshape(2, rows // 2, 2, cols // 2, 2, lat)
    patches = blocks.transpose(1, 3, 0, 2, 4, 5).reshape(tok, 8 * lat)

    patches, first, second, first_behind, second_ahead = lax.optimization_barrier(
        (patches, first, second, first_behind, second_ahead)
    )
    first_ahead, second_behind = ring(first, 1), ring(second, -1)
    first_opposite, second_opposite = ring(first_behind, -1), ring(second_ahead, 1)

    vmem = pl.BlockSpec(memory_space=pltpu.VMEM)
    params = pltpu.CompilerParams(vmem_limit_bytes=VMEM_BYTES)
    outgoing = pl.pallas_call(
        dispatch_kernel,
        out_shape=jax.ShapeDtypeStruct((slots, width), BF),
        in_specs=[pl.BlockSpec(memory_space=pltpu.SMEM)] + [vmem] * 5,
        out_specs=vmem,
        scratch_shapes=[pltpu.VMEM((16, *near.shape[1:]), BF)],
        compiler_params=params,
    )(lax.axis_index(FRAME).astype(jnp.int32).reshape(1), near, far, patches, context, table)

    arrived = lax.cond(
        lax.axis_index("yh") < 2,
        lambda block: lax.all_to_all(block, SOURCES, split_axis=0, concat_axis=0, tiled=True),
        lambda block: block,
        outgoing.reshape(experts, capacity, width),
    )
    mine = arrived.reshape(slots, width)
    theirs = lax.ppermute(mine, "c", SWAP)
    router = lax.dynamic_index_in_dim(router_weight, lax.axis_index("yh"), 0, keepdims=False)
    inputs, score = pl.pallas_call(
        turn_kernel,
        out_shape=[jax.ShapeDtypeStruct((width, 2 * slots), BF), jax.ShapeDtypeStruct((2 * slots, 1), F32)],
        in_specs=[vmem] * 3,
        out_specs=[vmem] * 2,
        compiler_params=params,
    )(mine, theirs, router.reshape(1, width))

    other, own = pl.pallas_call(
        expert_kernel,
        out_shape=[jax.ShapeDtypeStruct((slots, width), BF)] * 2,
        in_specs=[vmem] * 11,
        out_specs=[vmem] * 2,
        scratch_shapes=[pltpu.VMEM((2 * slots, 4 * share), BF), pltpu.VMEM((4 * share, width), BF)],
        compiler_params=params,
    )(inputs, score, gate, up, down, first_behind, first_ahead, first_opposite, second_behind, second_ahead, second_opposite)

    back = lax.ppermute(other, "c", SWAP)
    summed = (back.astype(F32) + own.astype(F32)).astype(BF).reshape(experts, capacity, width)
    homeward = lax.all_to_all(summed, SOURCES, split_axis=0, concat_axis=0, tiled=True)
    return dot(table, homeward.reshape(slots, width)).astype(BF)


def solution(mesh):
    fine = Mesh(mesh.devices.reshape(SIZES), NAMES)
    return jax.shard_map(
        local,
        mesh=fine,
        in_specs=(
            P(FRAME, EXPERT, None, None),
            P(),
            P(),
            P(None, FRAME),
            P((*FRAME, *EXPERT), None),
            P(None, None, EXPERT),
            P(EXPERT, None, FRAME),
            P(EXPERT, None, FRAME),
            P(EXPERT, FRAME, None),
            P((*FRAME, *EXPERT), None),
        ),
        out_specs=P((*FRAME, *EXPERT), None),
        check_vma=False,
    )
```

```python
import jax
import jax.numpy as jnp
from jax import lax
from jax.experimental import pallas as pl
from jax.experimental.pallas import tpu as pltpu
from jax.sharding import Mesh, PartitionSpec as P

FRAME = ("yh", "x", "c")
EXPERT = ("yl", "z")
SOURCES = ("yh", "yl", "z")
SIZES = (2, 4, 2, 4, 8)
NAMES = ("yh", "x", "c", "yl", "z")
BF = jnp.bfloat16
F32 = jnp.float32
SWAP = [(0, 1), (1, 0)]
XOR1 = [(i, i ^ 1) for i in range(4)]
XOR3 = [(i, i ^ 3) for i in range(4)]
VMEM_BYTES = 16 * 1024 * 1024
WIDE_BYTES = 65_600_000


def dot(a, b, dims=((1,), (0,))):
    return lax.dot_general(a, b, (dims, ((), ())), preferred_element_type=F32)


def shifted(value, axes, step):
    count = lax.axis_size(axes)
    pairs = [(i, i + step) for i in range(count) if 0 <= i + step < count]
    return lax.ppermute(value, axes, pairs)


def encode(video, past, conv_weight, latent_weight):
    frames, rows, cols, chans = video.shape
    stacked = jnp.concatenate([past, video], axis=0)
    above = shifted(stacked[:, rows - 1 :], EXPERT, 1)
    below = shifted(stacked[:, :1], EXPERT, -1)
    tall = jnp.concatenate([above, stacked, below], axis=1)

    def windows(block):
        wide = jnp.pad(block, ((0, 0), (0, 0), (1, 1), (0, 0)))
        taps = [wide[:, b : b + rows, q : q + cols] for b in range(3) for q in range(3)]
        return jnp.concatenate(taps, axis=-1).reshape(block.shape[0], rows * cols, 9 * chans)

    kernel = conv_weight.reshape(3, 9 * chans, chans)
    seen = windows(tall)
    mixed = sum(dot(seen[a : a + frames].reshape(-1, 9 * chans), kernel[a]) for a in range(3))
    feature = (video.reshape(-1, chans).astype(F32) + jax.nn.silu(mixed)).astype(BF)
    return dot(feature, latent_weight).astype(BF)


def place_table(routes, experts, capacity):
    tok = routes.shape[0]
    flat = routes.reshape(-1)
    count = flat.shape[0]
    chosen = (flat[:, None] == jnp.arange(experts, dtype=jnp.int32)[None, :]).astype(BF)
    at = jnp.arange(count, dtype=jnp.int32)
    before = (at[:, None] > at[None, :]).astype(BF)
    rank = jnp.sum(dot(before, chosen) * chosen.astype(F32), axis=1).astype(jnp.int32)
    place = jnp.where(rank < capacity, flat * capacity + rank, -1).reshape(tok, 2)
    slots = jnp.arange(experts * capacity, dtype=jnp.int32)[None, :]
    hit = (place[:, :1] == slots) | (place[:, 1:] == slots)
    return hit.astype(BF)


def pack_kernel(gate_ref, up_ref, down_ref, out_ref, sems):
    share = down_ref.shape[0]
    copies = [
        pltpu.make_async_copy(ref, out_ref.at[pl.ds(i * share, share)], sems.at[i])
        for i, ref in enumerate((gate_ref, up_ref, down_ref))
    ]
    for copy in copies:
        copy.start()
    for copy in copies:
        copy.wait()


def dispatch_kernel(patches_ref, context_ref, table_ref, out_ref):
    width = context_ref.shape[1]
    table = table_ref[...]
    out_ref[:, :width] = dot(table, context_ref[...], ((0,), (0,))).astype(BF)
    out_ref[:, width:] = dot(table, patches_ref[...], ((0,), (0,))).astype(BF)


def embed_kernel(at_ref, parts_ref, out_ref):
    yh, x, c = at_ref[0], at_ref[1], at_ref[2]
    size = parts_ref.shape[1]
    for shard in range(16):
        apart = shard // 2 % 4 ^ x
        mirror = apart // 2
        at = (apart % 2 ^ mirror) + mirror * 2 + (shard // 8 ^ yh) * 4 + (shard % 2 ^ c) * 8
        out_ref[shard * size : (shard + 1) * size] = parts_ref[at]


def expert_kernel(rows_ref, embed_ref, router_ref, w0_ref, w1_ref, w2_ref, w3_ref, out_ref, held_ref, sems):
    width = out_ref.shape[1]
    share = w0_ref.shape[0] // 3
    copies = [
        pltpu.make_async_copy(ref, held_ref.at[i], sems.at[i])
        for i, ref in enumerate((w0_ref, w1_ref, w2_ref, w3_ref))
    ]
    for copy in copies:
        copy.start()
    embedded = dot(rows_ref[:, width:], embed_ref[...], ((1,), (1,))).astype(BF)
    total = embedded.astype(F32) + rows_ref[:, :width].astype(F32)
    meansq = jnp.mean(total * total, axis=1, keepdims=True)
    tokens = (total * lax.rsqrt(meansq + 1e-06)).astype(BF)
    logit = jnp.sum(tokens.astype(F32) * router_ref[...].astype(F32), axis=1, keepdims=True)
    score = 1.0 / (1.0 + jnp.exp(-logit))
    hidden = []
    for i, copy in enumerate(copies):
        copy.wait()
        both = dot(tokens, held_ref[i, : 2 * share], ((1,), (1,)))
        gate, up = both[:, :share], both[:, share:]
        hidden.append((gate / (1.0 + jnp.exp(-gate)) * up).astype(BF))
    hidden = jnp.concatenate(hidden, axis=1)
    tile = 512
    for at in range(0, width, tile):
        down = jnp.concatenate([held_ref[i, 2 * share :, at : at + tile] for i in range(4)], axis=0)
        out_ref[:, at : at + tile] = (dot(hidden, down) * score).astype(BF)


def local(
    video,
    conv_weight,
    latent_weight,
    embed_weight,
    context,
    router_weight,
    gate_weight,
    up_weight,
    down_weight,
    routes,
):
    rows, cols = video.shape[1:3]
    tok, width = context.shape
    experts, capacity = 64, 2
    slots = experts * capacity
    share = down_weight.shape[1]
    hbm = pl.BlockSpec(memory_space=pltpu.HBM)
    vmem = pl.BlockSpec(memory_space=pltpu.VMEM)
    smem = pl.BlockSpec(memory_space=pltpu.SMEM)
    params = pltpu.CompilerParams(vmem_limit_bytes=VMEM_BYTES)

    past = shifted(video, FRAME, 1)
    held = pl.pallas_call(
        pack_kernel,
        out_shape=jax.ShapeDtypeStruct((3 * share, width), BF),
        in_specs=[hbm] * 3,
        out_specs=hbm,
        scratch_shapes=[pltpu.SemaphoreType.DMA((3,))],
        compiler_params=params,
    )(gate_weight[0].T, up_weight[0].T, down_weight[0])
    parts = embed_weight.T[None]
    for axis, pairs in (("x", XOR1), ("x", XOR3)):
        parts = jnp.concatenate([parts, lax.ppermute(parts, axis, pairs)], axis=0)
    held, past, parts = lax.optimization_barrier((held, past, parts))
    across = lax.ppermute(held, "x", XOR1)
    beside = lax.ppermute(held, "c", SWAP)

    table = place_table(routes, experts, capacity)
    latent = encode(video, past, conv_weight, latent_weight)
    lat = latent.shape[1]
    blocks = latent.reshape(2, rows // 2, 2, cols // 2, 2, lat)
    patches = blocks.transpose(1, 3, 0, 2, 4, 5).reshape(tok, 8 * lat)
    for axis in ("yh", "c"):
        parts = jnp.concatenate([parts, lax.ppermute(parts, axis, SWAP)], axis=0)
    patches, parts = lax.optimization_barrier((patches, parts))
    raw = width + patches.shape[1]
    outgoing = pl.pallas_call(
        dispatch_kernel,
        out_shape=jax.ShapeDtypeStruct((slots, raw), BF),
        in_specs=[vmem] * 3,
        out_specs=vmem,
        compiler_params=pltpu.CompilerParams(vmem_limit_bytes=WIDE_BYTES),
    )(patches, context, table)

    arrived = lax.all_to_all(outgoing.reshape(experts, capacity, raw), SOURCES, split_axis=0, concat_axis=0, tiled=True)
    mine = arrived.reshape(slots, raw)
    theirs = lax.ppermute(mine, "x", XOR3)
    across, mine = lax.optimization_barrier((across, mine))
    corner = lax.ppermute(across, "c", SWAP)
    weights = (held, beside, across, corner)

    embed = pl.pallas_call(
        embed_kernel,
        out_shape=jax.ShapeDtypeStruct((width, parts.shape[2]), BF),
        in_specs=[smem, vmem],
        out_specs=vmem,
        compiler_params=params,
    )(jnp.stack([lax.axis_index(axis) for axis in FRAME]).astype(jnp.int32), parts)

    router = lax.dynamic_index_in_dim(router_weight, lax.axis_index("yh"), 0, keepdims=False).reshape(1, width)

    def expert(block):
        return pl.pallas_call(
            expert_kernel,
            out_shape=jax.ShapeDtypeStruct((slots, width), BF),
            in_specs=[vmem] * 3 + [hbm] * 4,
            out_specs=vmem,
            scratch_shapes=[pltpu.VMEM((4, 3 * share, width), BF), pltpu.SemaphoreType.DMA((4,))],
            compiler_params=params,
        )(block, embed, router, *weights)

    back = lax.ppermute(expert(theirs), "x", XOR3)
    own = expert(mine)
    summed = (back.astype(F32) + own.astype(F32)).astype(BF).reshape(experts, capacity, width)
    homeward = lax.all_to_all(summed, SOURCES, split_axis=0, concat_axis=0, tiled=True)
    return dot(table, homeward.reshape(slots, width)).astype(BF)


def solution(mesh):
    fine = Mesh(mesh.devices.reshape(SIZES), NAMES)
    return jax.shard_map(
        local,
        mesh=fine,
        in_specs=(
            P(FRAME, EXPERT, None, None),
            P(),
            P(),
            P(None, FRAME),
            P((*FRAME, *EXPERT), None),
            P(None, None, EXPERT),
            P(EXPERT, None, FRAME),
            P(EXPERT, None, FRAME),
            P(EXPERT, FRAME, None),
            P((*FRAME, *EXPERT), None),
        ),
        out_specs=P((*FRAME, *EXPERT), None),
        check_vma=False,
    )
```

```python
import jax
import jax.numpy as jnp
from jax import lax
from jax.experimental import pallas as pl
from jax.experimental.pallas import tpu as pltpu
from jax.sharding import Mesh, PartitionSpec as P

FRAME = ("yh", "x", "c")
EXPERT = ("yl", "z")
SOURCES = ("yh", "yl", "z")
SIZES = (2, 4, 2, 4, 8)
NAMES = ("yh", "x", "c", "yl", "z")
BF = jnp.bfloat16
F32 = jnp.float32
SWAP = [(0, 1), (1, 0)]
XOR1 = [(i, i ^ 1) for i in range(4)]
XOR3 = [(i, i ^ 3) for i in range(4)]
VMEM_BYTES = 16 * 1024 * 1024
WIDE_BYTES = 65_600_000


def dot(a, b, dims=((1,), (0,))):
    return lax.dot_general(a, b, (dims, ((), ())), preferred_element_type=F32)


def shifted(value, axes, step):
    count = lax.axis_size(axes)
    pairs = [(i, i + step) for i in range(count) if 0 <= i + step < count]
    return lax.ppermute(value, axes, pairs)


def ring(value, step):
    return lax.ppermute(value, "x", [(i, (i - step) % 4) for i in range(4)])


def encode(video, past, conv_weight, latent_weight):
    frames, rows, cols, chans = video.shape
    stacked = jnp.concatenate([past, video], axis=0)
    above = shifted(stacked[:, rows - 1 :], EXPERT, 1)
    below = shifted(stacked[:, :1], EXPERT, -1)
    tall = jnp.concatenate([above, stacked, below], axis=1)

    def windows(block):
        wide = jnp.pad(block, ((0, 0), (0, 0), (1, 1), (0, 0)))
        taps = [wide[:, b : b + rows, q : q + cols] for b in range(3) for q in range(3)]
        return jnp.concatenate(taps, axis=-1).reshape(block.shape[0], rows * cols, 9 * chans)

    kernel = conv_weight.reshape(3, 9 * chans, chans)
    seen = windows(tall)
    mixed = sum(dot(seen[a : a + frames].reshape(-1, 9 * chans), kernel[a]) for a in range(3))
    feature = (video.reshape(-1, chans).astype(F32) + jax.nn.silu(mixed)).astype(BF)
    return dot(feature, latent_weight).astype(BF)


def place_table(routes, experts, capacity):
    tok = routes.shape[0]
    flat = routes.reshape(-1)
    count = flat.shape[0]
    chosen = (flat[:, None] == jnp.arange(experts, dtype=jnp.int32)[None, :]).astype(BF)
    at = jnp.arange(count, dtype=jnp.int32)
    before = (at[:, None] > at[None, :]).astype(BF)
    rank = jnp.sum(dot(before, chosen) * chosen.astype(F32), axis=1).astype(jnp.int32)
    place = jnp.where(rank < capacity, flat * capacity + rank, -1).reshape(tok, 2)
    slots = jnp.arange(experts * capacity, dtype=jnp.int32)[None, :]
    hit = (place[:, :1] == slots) | (place[:, 1:] == slots)
    return hit.astype(BF)


def pack_kernel(gate_ref, up_ref, down_ref, out_ref, sems):
    share = down_ref.shape[0]
    copies = [
        pltpu.make_async_copy(ref, out_ref.at[pl.ds(i * share, share)], sems.at[i])
        for i, ref in enumerate((gate_ref, up_ref, down_ref))
    ]
    for copy in copies:
        copy.start()
    for copy in copies:
        copy.wait()


def dispatch_kernel(patches_ref, context_ref, table_ref, out_ref):
    width = context_ref.shape[1]
    table = table_ref[...]
    out_ref[:, :width] = dot(table, context_ref[...], ((0,), (0,))).astype(BF)
    out_ref[:, width:] = dot(table, patches_ref[...], ((0,), (0,))).astype(BF)


def embed_kernel(at_ref, parts_ref, out_ref):
    yh, x, c = at_ref[0], at_ref[1], at_ref[2]
    size = parts_ref.shape[1]
    for shard in range(16):
        apart = shard // 2 % 4 ^ x
        mirror = apart // 2
        at = mirror * 8 + (apart % 2 ^ mirror) * 4 + (shard % 2 ^ c) * 2 + (shard // 8 ^ yh)
        out_ref[shard * size : (shard + 1) * size] = parts_ref[at]


def silu(value):
    return value / (1.0 + jnp.exp(-value))


def near_kernel(
    mine_ref, theirs_ref, embed_ref, router_ref, w0_ref, w1_ref, w2_ref, tokens_ref, score_ref, total_ref, held_ref, sems
):
    rows, width = mine_ref.shape[0], total_ref.shape[1]
    share = w0_ref.shape[0] // 3
    copies = [pltpu.make_async_copy(ref, held_ref.at[i], sems.at[i]) for i, ref in enumerate((w0_ref, w1_ref, w2_ref))]
    for copy in copies:
        copy.start()
    for half, ref in enumerate((theirs_ref, mine_ref)):
        embedded = dot(ref[:, width:], embed_ref[...], ((1,), (1,))).astype(BF)
        total = embedded.astype(F32) + ref[:, :width].astype(F32)
        meansq = jnp.mean(total * total, axis=1, keepdims=True)
        tokens = (total * lax.rsqrt(meansq + 1e-06)).astype(BF)
        logit = jnp.sum(tokens.astype(F32) * router_ref[...].astype(F32), axis=1, keepdims=True)
        at = slice(half * rows, (half + 1) * rows)
        tokens_ref[at] = tokens
        score_ref[at] = 1.0 / (1.0 + jnp.exp(-logit))
    hidden = []
    for i, copy in enumerate(copies):
        copy.wait()
        both = dot(tokens_ref[...], held_ref[i, : 2 * share], ((1,), (1,)))
        hidden.append((silu(both[:, :share]) * both[:, share:]).astype(BF))
    hidden = jnp.concatenate(hidden, axis=1)
    tile = 512
    for at in range(0, width, tile):
        down = jnp.concatenate([held_ref[i, 2 * share :, at : at + tile] for i in range(3)], axis=0)
        total_ref[:, at : at + tile] = dot(hidden, down)


def last_kernel(tokens_ref, score_ref, total_ref, w0_ref, w1_ref, other_ref, own_ref, held_ref, sems):
    rows, width = other_ref.shape
    part, share = w0_ref.shape[0], held_ref.shape[0] // 3
    copies = [
        pltpu.make_async_copy(ref, held_ref.at[pl.ds(i * part, part)], sems.at[i]) for i, ref in enumerate((w0_ref, w1_ref))
    ]
    for copy in copies:
        copy.start()
    for copy in copies:
        copy.wait()
    both = dot(tokens_ref[...], held_ref[: 2 * share], ((1,), (1,)))
    hidden = (silu(both[:, :share]) * both[:, share:]).astype(BF)
    tile = 512
    for at in range(0, width, tile):
        cut = slice(at, at + tile)
        total = total_ref[:, cut] + dot(hidden, held_ref[2 * share :, cut])
        total = (total * score_ref[...]).astype(BF)
        other_ref[:, cut] = total[:rows]
        own_ref[:, cut] = total[rows:]


def local(
    video,
    conv_weight,
    latent_weight,
    embed_weight,
    context,
    router_weight,
    gate_weight,
    up_weight,
    down_weight,
    routes,
):
    rows, cols = video.shape[1:3]
    tok, width = context.shape
    experts, capacity = 64, 2
    slots = experts * capacity
    share = down_weight.shape[1]
    hbm = pl.BlockSpec(memory_space=pltpu.HBM)
    vmem = pl.BlockSpec(memory_space=pltpu.VMEM)
    smem = pl.BlockSpec(memory_space=pltpu.SMEM)
    params = pltpu.CompilerParams(vmem_limit_bytes=VMEM_BYTES)

    past = shifted(video, FRAME, 1)
    held = pl.pallas_call(
        pack_kernel,
        out_shape=jax.ShapeDtypeStruct((3 * share, width), BF),
        in_specs=[hbm] * 3,
        out_specs=hbm,
        scratch_shapes=[pltpu.SemaphoreType.DMA((3,))],
        compiler_params=params,
    )(gate_weight[0].T, up_weight[0].T, down_weight[0])
    held, past = lax.optimization_barrier((held, past))
    behind, ahead = ring(held, -1), ring(held, 1)

    table = place_table(routes, experts, capacity)
    latent = encode(video, past, conv_weight, latent_weight)
    lat = latent.shape[1]
    blocks = latent.reshape(2, rows // 2, 2, cols // 2, 2, lat)
    patches = blocks.transpose(1, 3, 0, 2, 4, 5).reshape(tok, 8 * lat)
    raw = width + patches.shape[1]
    outgoing = pl.pallas_call(
        dispatch_kernel,
        out_shape=jax.ShapeDtypeStruct((slots, raw), BF),
        in_specs=[vmem] * 3,
        out_specs=vmem,
        compiler_params=params,
    )(patches, context, table)

    arrived = lax.all_to_all(outgoing.reshape(experts, capacity, raw), SOURCES, split_axis=0, concat_axis=0, tiled=True)
    parts = embed_weight.T[None]
    for axis, pairs in (("yh", SWAP), ("c", SWAP), ("x", XOR1), ("x", XOR3)):
        parts = jnp.concatenate([parts, lax.ppermute(parts, axis, pairs)], axis=0)
    part = 3 * share // 2
    arrived, parts, first, second = lax.optimization_barrier((arrived, parts, behind[:part], ahead[part:]))
    first, second = ring(first, -1), ring(second, 1)

    mine = arrived.reshape(slots, raw)
    theirs = lax.ppermute(mine, "c", SWAP)
    embed = pl.pallas_call(
        embed_kernel,
        out_shape=jax.ShapeDtypeStruct((width, parts.shape[2]), BF),
        in_specs=[smem, vmem],
        out_specs=vmem,
        compiler_params=pltpu.CompilerParams(vmem_limit_bytes=WIDE_BYTES),
    )(jnp.stack([lax.axis_index(axis) for axis in FRAME]).astype(jnp.int32), parts)

    router = lax.dynamic_index_in_dim(router_weight, lax.axis_index("yh"), 0, keepdims=False).reshape(1, width)

    tokens, score, total = pl.pallas_call(
        near_kernel,
        out_shape=[
            jax.ShapeDtypeStruct((2 * slots, width), BF),
            jax.ShapeDtypeStruct((2 * slots, 1), F32),
            jax.ShapeDtypeStruct((2 * slots, width), F32),
        ],
        in_specs=[vmem] * 4 + [hbm] * 3,
        out_specs=[vmem] * 3,
        scratch_shapes=[pltpu.VMEM((3, 3 * share, width), BF), pltpu.SemaphoreType.DMA((3,))],
        compiler_params=params,
    )(mine, theirs, embed, router, held, behind, ahead)
    other, own = pl.pallas_call(
        last_kernel,
        out_shape=[jax.ShapeDtypeStruct((slots, width), BF)] * 2,
        in_specs=[vmem] * 3 + [hbm] * 2,
        out_specs=[vmem] * 2,
        scratch_shapes=[pltpu.VMEM((3 * share, width), BF), pltpu.SemaphoreType.DMA((2,))],
        compiler_params=params,
    )(tokens, score, total, first, second)
    back = lax.ppermute(other, "c", SWAP)
    summed = (back.astype(F32) + own.astype(F32)).astype(BF).reshape(experts, capacity, width)
    homeward = lax.all_to_all(summed, SOURCES, split_axis=0, concat_axis=0, tiled=True)
    return dot(table, homeward.reshape(slots, width)).astype(BF)


def solution(mesh):
    fine = Mesh(mesh.devices.reshape(SIZES), NAMES)
    return jax.shard_map(
        local,
        mesh=fine,
        in_specs=(
            P(FRAME, EXPERT, None, None),
            P(),
            P(),
            P(None, FRAME),
            P((*FRAME, *EXPERT), None),
            P(None, None, EXPERT),
            P(EXPERT, None, FRAME),
            P(EXPERT, None, FRAME),
            P(EXPERT, FRAME, None),
            P((*FRAME, *EXPERT), None),
        ),
        out_specs=P((*FRAME, *EXPERT), None),
        check_vma=False,
    )
```

```python
import jax
import jax.numpy as jnp
from jax import lax
from jax.experimental import pallas as pl
from jax.experimental.pallas import tpu as pltpu
from jax.sharding import Mesh, PartitionSpec as P

FRAME = ("yh", "x", "c")
EXPERT = ("yl", "z")
SOURCES = ("yh", "yl", "z")
SIZES = (2, 4, 2, 4, 8)
NAMES = ("yh", "x", "c", "yl", "z")
BF = jnp.bfloat16
F32 = jnp.float32
SWAP = [(0, 1), (1, 0)]
VMEM_BYTES = 16 * 1024 * 1024
WIDE_BYTES = 65_600_000


def dot(a, b, dims=((1,), (0,))):
    return lax.dot_general(a, b, (dims, ((), ())), preferred_element_type=F32)


def shifted(value, axes, step):
    count = lax.axis_size(axes)
    pairs = [(i, i + step) for i in range(count) if 0 <= i + step < count]
    return lax.ppermute(value, axes, pairs)


def ring(value, step):
    return lax.ppermute(value, "x", [(i, (i - step) % 4) for i in range(4)])


def encode(video, past, conv_weight, latent_weight):
    frames, rows, cols, chans = video.shape
    stacked = jnp.concatenate([past, video], axis=0)
    above = shifted(stacked[:, rows - 1 :], EXPERT, 1)
    below = shifted(stacked[:, :1], EXPERT, -1)
    tall = jnp.concatenate([above, stacked, below], axis=1)

    def windows(block):
        wide = jnp.pad(block, ((0, 0), (0, 0), (1, 1), (0, 0)))
        taps = [wide[:, b : b + rows, q : q + cols] for b in range(3) for q in range(3)]
        return jnp.concatenate(taps, axis=-1).reshape(block.shape[0], rows * cols, 9 * chans)

    kernel = conv_weight.reshape(3, 9 * chans, chans)
    seen = windows(tall)
    mixed = sum(dot(seen[a : a + frames].reshape(-1, 9 * chans), kernel[a]) for a in range(3))
    feature = (video.reshape(-1, chans).astype(F32) + jax.nn.silu(mixed)).astype(BF)
    return dot(feature, latent_weight).astype(BF)


def place_table(routes, experts, capacity):
    tok = routes.shape[0]
    flat = routes.reshape(-1)
    count = flat.shape[0]
    chosen = (flat[:, None] == jnp.arange(experts, dtype=jnp.int32)[None, :]).astype(BF)
    at = jnp.arange(count, dtype=jnp.int32)
    before = (at[:, None] > at[None, :]).astype(BF)
    rank = jnp.sum(dot(before, chosen) * chosen.astype(F32), axis=1).astype(jnp.int32)
    place = jnp.where(rank < capacity, flat * capacity + rank, -1).reshape(tok, 2)
    slots = jnp.arange(experts * capacity, dtype=jnp.int32)[None, :]
    hit = (place[:, :1] == slots) | (place[:, 1:] == slots)
    return hit.astype(BF)


def pack_kernel(gate_ref, up_ref, down_ref, first_ref, second_ref, sems):
    share = down_ref.shape[0]
    half = share // 2
    copies = [
        pltpu.make_async_copy(gate_ref, first_ref.at[pl.ds(0, share)], sems.at[0]),
        pltpu.make_async_copy(up_ref.at[pl.ds(0, half)], first_ref.at[pl.ds(share, half)], sems.at[1]),
        pltpu.make_async_copy(up_ref.at[pl.ds(half, half)], second_ref.at[pl.ds(0, half)], sems.at[2]),
        pltpu.make_async_copy(down_ref, second_ref.at[pl.ds(half, share)], sems.at[3]),
    ]
    for copy in copies:
        copy.start()
    for copy in copies:
        copy.wait()


def dispatch_kernel(patches_ref, context_ref, table_ref, out_ref):
    width = context_ref.shape[1]
    table = table_ref[...]
    out_ref[:, :width] = dot(table, context_ref[...], ((0,), (0,))).astype(BF)
    out_ref[:, width:] = dot(table, patches_ref[...], ((0,), (0,))).astype(BF)


def embed_kernel(at_ref, parts_ref, out_ref):
    yh, x, c = at_ref[0], at_ref[1], at_ref[2]
    size = parts_ref.shape[1]
    for shard in range(16):
        at = lax.rem(shard // 2 % 4 - x + 4, 4) + (shard // 8 ^ yh) * 4 + (shard % 2 ^ c) * 8
        out_ref[shard * size : (shard + 1) * size] = parts_ref[at]


def silu(value):
    return value / (1.0 + jnp.exp(-value))


def near_kernel(
    mine_ref, theirs_ref, embed_ref, router_ref, a0_ref, b0_ref, a1_ref, b1_ref, a2_ref, b2_ref, tokens_ref, score_ref, total_ref, held_ref, sems
):
    rows, width = mine_ref.shape[0], total_ref.shape[1]
    part, share = a0_ref.shape[0], held_ref.shape[1] // 3
    copies = [
        pltpu.make_async_copy(ref, held_ref.at[i // 2, pl.ds(i % 2 * part, part)], sems.at[i])
        for i, ref in enumerate((a0_ref, b0_ref, a1_ref, b1_ref, a2_ref, b2_ref))
    ]
    for copy in copies:
        copy.start()
    for half, ref in enumerate((theirs_ref, mine_ref)):
        embedded = dot(ref[:, width:], embed_ref[...], ((1,), (1,))).astype(BF)
        total = embedded.astype(F32) + ref[:, :width].astype(F32)
        meansq = jnp.mean(total * total, axis=1, keepdims=True)
        tokens = (total * lax.rsqrt(meansq + 1e-06)).astype(BF)
        logit = jnp.sum(tokens.astype(F32) * router_ref[...].astype(F32), axis=1, keepdims=True)
        at = slice(half * rows, (half + 1) * rows)
        tokens_ref[at] = tokens
        score_ref[at] = 1.0 / (1.0 + jnp.exp(-logit))
    hidden = []
    for i in range(3):
        copies[2 * i].wait()
        copies[2 * i + 1].wait()
        both = dot(tokens_ref[...], held_ref[i, : 2 * share], ((1,), (1,)))
        hidden.append((silu(both[:, :share]) * both[:, share:]).astype(BF))
    hidden = jnp.concatenate(hidden, axis=1)
    tile = 512
    for at in range(0, width, tile):
        down = jnp.concatenate([held_ref[i, 2 * share :, at : at + tile] for i in range(3)], axis=0)
        total_ref[:, at : at + tile] = dot(hidden, down)


def last_kernel(tokens_ref, score_ref, total_ref, w0_ref, w1_ref, other_ref, own_ref, held_ref, sems):
    rows, width = other_ref.shape
    part, share = w0_ref.shape[0], held_ref.shape[0] // 3
    copies = [
        pltpu.make_async_copy(ref, held_ref.at[pl.ds(i * part, part)], sems.at[i]) for i, ref in enumerate((w0_ref, w1_ref))
    ]
    for copy in copies:
        copy.start()
    for copy in copies:
        copy.wait()
    both = dot(tokens_ref[...], held_ref[: 2 * share], ((1,), (1,)))
    hidden = (silu(both[:, :share]) * both[:, share:]).astype(BF)
    tile = 512
    for at in range(0, width, tile):
        cut = slice(at, at + tile)
        total = total_ref[:, cut] + dot(hidden, held_ref[2 * share :, cut])
        total = (total * score_ref[...]).astype(BF)
        other_ref[:, cut] = total[:rows]
        own_ref[:, cut] = total[rows:]


def local(
    video,
    conv_weight,
    latent_weight,
    embed_weight,
    context,
    router_weight,
    gate_weight,
    up_weight,
    down_weight,
    routes,
):
    rows, cols = video.shape[1:3]
    tok, width = context.shape
    experts, capacity = 64, 2
    slots = experts * capacity
    share = down_weight.shape[1]
    hbm = pl.BlockSpec(memory_space=pltpu.HBM)
    vmem = pl.BlockSpec(memory_space=pltpu.VMEM)
    smem = pl.BlockSpec(memory_space=pltpu.SMEM)
    params = pltpu.CompilerParams(vmem_limit_bytes=VMEM_BYTES)

    past = shifted(video, FRAME, 1)
    part = embed_weight.T
    parts = jnp.stack([part, ring(part, 1), ring(part, 2), ring(part, 3)])
    first, second = pl.pallas_call(
        pack_kernel,
        out_shape=[jax.ShapeDtypeStruct((3 * share // 2, width), BF)] * 2,
        in_specs=[hbm] * 3,
        out_specs=[hbm] * 2,
        scratch_shapes=[pltpu.SemaphoreType.DMA((4,))],
        compiler_params=params,
    )(gate_weight[0].T, up_weight[0].T, down_weight[0])
    first, second, past, parts = lax.optimization_barrier((first, second, past, parts))
    first_behind, second_ahead = ring(first, -1), ring(second, 1)
    first_ahead, second_behind = ring(first, 1), ring(second, -1)

    table = place_table(routes, experts, capacity)
    raw = width + embed_weight.shape[0]

    def front(video, past, conv_weight, latent_weight, context, table):
        latent = encode(video, past, conv_weight, latent_weight)
        lat = latent.shape[1]
        blocks = latent.reshape(2, rows // 2, 2, cols // 2, 2, lat)
        patches = blocks.transpose(1, 3, 0, 2, 4, 5).reshape(tok, 8 * lat)
        return pl.pallas_call(
            dispatch_kernel,
            out_shape=jax.ShapeDtypeStruct((slots, raw), BF),
            in_specs=[vmem] * 3,
            out_specs=vmem,
            compiler_params=params,
        )(patches, context, table).reshape(experts, capacity, raw)

    outgoing = lax.cond(
        lax.axis_index("yh") < 2,
        front,
        lambda *unused: jnp.zeros((experts, capacity, raw), BF),
        video,
        past,
        conv_weight,
        latent_weight,
        context,
        table,
    )
    arrived = lax.all_to_all(outgoing, SOURCES, split_axis=0, concat_axis=0, tiled=True)
    parts = jnp.concatenate([parts, lax.ppermute(parts, "yh", SWAP)], axis=0)
    parts, first_behind, second_ahead = lax.optimization_barrier((parts, first_behind, second_ahead))
    first_opposite, second_opposite = ring(first_behind, -1), ring(second_ahead, 1)
    parts = jnp.concatenate([parts, lax.ppermute(parts, "c", SWAP)], axis=0)
    arrived, parts, first_ahead, second_behind = lax.optimization_barrier((arrived, parts, first_ahead, second_behind))

    mine = arrived.reshape(slots, raw)
    theirs = lax.ppermute(mine, "c", SWAP)
    embed = pl.pallas_call(
        embed_kernel,
        out_shape=jax.ShapeDtypeStruct((width, parts.shape[2]), BF),
        in_specs=[smem, vmem],
        out_specs=vmem,
        compiler_params=pltpu.CompilerParams(vmem_limit_bytes=WIDE_BYTES),
    )(jnp.stack([lax.axis_index(axis) for axis in FRAME]).astype(jnp.int32), parts)

    router = lax.dynamic_index_in_dim(router_weight, lax.axis_index("yh"), 0, keepdims=False).reshape(1, width)

    tokens, score, total = pl.pallas_call(
        near_kernel,
        out_shape=[
            jax.ShapeDtypeStruct((2 * slots, width), BF),
            jax.ShapeDtypeStruct((2 * slots, 1), F32),
            jax.ShapeDtypeStruct((2 * slots, width), F32),
        ],
        in_specs=[vmem] * 4 + [hbm] * 6,
        out_specs=[vmem] * 3,
        scratch_shapes=[pltpu.VMEM((3, 3 * share, width), BF), pltpu.SemaphoreType.DMA((6,))],
        compiler_params=params,
    )(mine, theirs, embed, router, first, second, first_behind, second_behind, first_ahead, second_ahead)
    other, own = pl.pallas_call(
        last_kernel,
        out_shape=[jax.ShapeDtypeStruct((slots, width), BF)] * 2,
        in_specs=[vmem] * 3 + [hbm] * 2,
        out_specs=[vmem] * 2,
        scratch_shapes=[pltpu.VMEM((3 * share, width), BF), pltpu.SemaphoreType.DMA((2,))],
        compiler_params=params,
    )(tokens, score, total, first_opposite, second_opposite)
    back = lax.ppermute(other, "c", SWAP)
    summed = (back.astype(F32) + own.astype(F32)).astype(BF).reshape(experts, capacity, width)
    homeward = lax.all_to_all(summed, SOURCES, split_axis=0, concat_axis=0, tiled=True)
    return dot(table, homeward.reshape(slots, width)).astype(BF)


def solution(mesh):
    fine = Mesh(mesh.devices.reshape(SIZES), NAMES)
    return jax.shard_map(
        local,
        mesh=fine,
        in_specs=(
            P(FRAME, EXPERT, None, None),
            P(),
            P(),
            P(None, FRAME),
            P((*FRAME, *EXPERT), None),
            P(None, None, EXPERT),
            P(EXPERT, None, FRAME),
            P(EXPERT, None, FRAME),
            P(EXPERT, FRAME, None),
            P((*FRAME, *EXPERT), None),
        ),
        out_specs=P((*FRAME, *EXPERT), None),
        check_vma=False,
    )
```

```python
import jax
import jax.numpy as jnp
from jax import lax
from jax.experimental import pallas as pl
from jax.experimental.pallas import tpu as pltpu
from jax.sharding import Mesh, PartitionSpec as P

FRAME = ("yh", "x", "c")
EXPERT = ("yl", "z")
SOURCES = ("yh", "yl", "z")
SIZES = (2, 4, 2, 4, 8)
NAMES = ("yh", "x", "c", "yl", "z")
BF = jnp.bfloat16
F32 = jnp.float32
SWAP = [(0, 1), (1, 0)]
XOR1 = [(i, i ^ 1) for i in range(4)]
XOR3 = [(i, i ^ 3) for i in range(4)]
VMEM_BYTES = 16 * 1024 * 1024
PACK_BYTES = 66_400_000


def dot(a, b, dims=((1,), (0,))):
    return lax.dot_general(a, b, (dims, ((), ())), preferred_element_type=F32)


def shifted(value, axes, step):
    count = lax.axis_size(axes)
    pairs = [(i, i + step) for i in range(count) if 0 <= i + step < count]
    return lax.ppermute(value, axes, pairs)


def silu(value):
    return value / (1.0 + jnp.exp(-value))


def pack_kernel(gate_ref, up_ref, down_ref, parts_ref, out_ref, sems):
    share, tall = down_ref.shape[0], parts_ref.shape[0] * 128 // down_ref.shape[1]
    copies = [(ref, out_ref.at[pl.ds(i * share, share)]) for i, ref in enumerate((gate_ref, up_ref, down_ref))]
    for j in range(parts_ref.shape[0] // tall):
        target = out_ref.at[pl.ds(3 * share, tall), pl.ds(j * 128, 128)]
        copies.append((parts_ref.at[pl.ds(j * tall, tall)], target))
    copies = [pltpu.make_async_copy(*pair, sems.at[i]) for i, pair in enumerate(copies)]
    for copy in copies:
        copy.start()
    for copy in copies:
        copy.wait()


def front_kernel(tall_ref, conv_ref, latent_ref, context_ref, routes_ref, out_ref, table_ref, wide_ref):
    frames, rows, cols, chans = tall_ref.shape
    tok, width = context_ref.shape
    slots = table_ref.shape[1]

    flat = tall_ref[...].reshape(frames * rows * cols, chans).astype(F32)
    column = lax.broadcasted_iota(jnp.int32, flat.shape, 0) % cols
    wide_ref[:, :chans] = jnp.where(column == 0, 0.0, pltpu.roll(flat, 1, 0)).astype(BF)
    wide_ref[:, chans : 2 * chans] = flat.astype(BF)
    wide_ref[:, 2 * chans :] = jnp.where(column == cols - 1, 0.0, pltpu.roll(flat, flat.shape[0] - 1, 0)).astype(BF)

    size = (rows - 2) * cols
    out_row = lax.broadcasted_iota(jnp.int32, (size, size), 0)
    kind, token = out_row // (size // 4), out_row % (size // 4)
    source = (token // (cols // 2) * 2 + kind // 2) * cols + token % (cols // 2) * 2 + kind % 2
    sort = (source == lax.broadcasted_iota(jnp.int32, (size, size), 1)).astype(BF)
    lat = latent_ref.shape[1] // 8
    lane = lax.broadcasted_iota(jnp.int32, latent_ref.shape, 1) // lat
    patches = jnp.zeros((tok, 8 * lat), F32)
    for frame in range(frames - 2):
        mixed = jnp.zeros((size, chans), F32)
        for a in range(3):
            for b in range(3):
                at = ((frame + a) * rows + b) * cols
                mixed += dot(wide_ref[at : at + size], conv_ref[a, b])
        video = tall_ref[frame + 2, 1 : rows - 1].reshape(size, chans).astype(F32)
        feature = (video + silu(mixed)).astype(BF)
        feature = dot(sort, feature).astype(BF)
        for part in range(4):
            weight = jnp.where(lane == frame * 4 + part, latent_ref[...], jnp.zeros((), BF))
            patches += dot(feature[part * tok : (part + 1) * tok], weight)
    patches = patches.astype(BF)

    slot = lax.broadcasted_iota(jnp.int32, (tok, slots), 1)
    chosen = (routes_ref[:, :1] == slot // 2) | (routes_ref[:, 1:] == slot // 2)
    order = [lax.broadcasted_iota(jnp.int32, (tok, tok), axis) for axis in (0, 1)]
    before = dot((order[0] > order[1]).astype(BF), chosen.astype(BF))
    table = (chosen & (before == (slot % 2).astype(F32))).astype(BF)
    table_ref[...] = table
    out_ref[:, :width] = dot(table, context_ref[...], ((0,), (0,))).astype(BF)
    out_ref[:, width:] = dot(table, patches, ((0,), (0,))).astype(BF)


def expert_kernel(at_ref, rows_ref, router_ref, w0_ref, w1_ref, w2_ref, w3_ref, out_ref, embed_ref):
    held = (w0_ref, w1_ref, w2_ref, w3_ref)
    yh, x, c = at_ref[0], at_ref[1], at_ref[2]
    width = out_ref.shape[1]
    size = embed_ref.shape[1]
    share = (w0_ref.shape[0] - 4 * size * 128 // width) // 3
    tall = 4 * size * 128 // width
    for i, ref in enumerate(held):
        for m in range(4):
            shard = (yh ^ m % 2) * 8 + (x ^ i // 2 ^ m // 2 * 3) * 2 + (c ^ i % 2)
            for j in range(size // tall):
                lane = (m * (size // tall) + j) * 128
                embed_ref[shard, j * tall : (j + 1) * tall] = ref[3 * share :, lane : lane + 128]
    embed = embed_ref[...].reshape(width, 128)
    embedded = dot(rows_ref[:, width:], embed, ((1,), (1,))).astype(BF)
    total = embedded.astype(F32) + rows_ref[:, :width].astype(F32)
    meansq = jnp.mean(total * total, axis=1, keepdims=True)
    tokens = (total * lax.rsqrt(meansq + 1e-06)).astype(BF)
    router = jnp.where(yh == 0, router_ref[:1], router_ref[1:]).astype(F32)
    score = 1.0 / (1.0 + jnp.exp(-jnp.sum(tokens.astype(F32) * router, axis=1, keepdims=True)))
    hidden = []
    for ref in held:
        both = dot(tokens, ref[: 2 * share], ((1,), (1,)))
        hidden.append((silu(both[:, :share]) * both[:, share:]).astype(BF))
    hidden = jnp.concatenate(hidden, axis=1)
    tile = 512
    for at in range(0, width, tile):
        down = jnp.concatenate([ref[2 * share : 3 * share, at : at + tile] for ref in held], axis=0)
        out_ref[:, at : at + tile] = (dot(hidden, down) * score).astype(BF)


def local(
    video,
    conv_weight,
    latent_weight,
    embed_weight,
    context,
    router_weight,
    gate_weight,
    up_weight,
    down_weight,
    routes,
):
    rows, cols = video.shape[1:3]
    tok, width = context.shape
    experts, capacity = 64, 2
    slots = experts * capacity
    share = down_weight.shape[1]
    hbm = pl.BlockSpec(memory_space=pltpu.HBM)
    vmem = pl.BlockSpec(memory_space=pltpu.VMEM)
    smem = pl.BlockSpec(memory_space=pltpu.SMEM)
    params = pltpu.CompilerParams(vmem_limit_bytes=VMEM_BYTES)

    past = shifted(video, FRAME, 1)
    parts = embed_weight.T
    for axis, pairs in (("yh", SWAP), ("x", XOR3)):
        parts = jnp.concatenate([parts, lax.ppermute(parts, axis, pairs)], axis=0)
    tall = parts.shape[0] * parts.shape[1] // width
    held = pl.pallas_call(
        pack_kernel,
        out_shape=jax.ShapeDtypeStruct((3 * share + tall, width), BF),
        in_specs=[hbm] * 4,
        out_specs=hbm,
        scratch_shapes=[pltpu.SemaphoreType.DMA((3 + width // 128,))],
        compiler_params=pltpu.CompilerParams(vmem_limit_bytes=PACK_BYTES),
    )(gate_weight[0].T, up_weight[0].T, down_weight[0], parts)
    held, past = lax.optimization_barrier((held, past))
    across = lax.ppermute(held, "x", XOR1)
    beside = lax.ppermute(held, "c", SWAP)

    stacked = jnp.concatenate([past, video], axis=0)
    above = shifted(stacked[:, rows - 1 :], EXPERT, 1)
    below = shifted(stacked[:, :1], EXPERT, -1)
    padded = jnp.concatenate([above, stacked, below], axis=1)
    chans = video.shape[3]
    raw = width + embed_weight.shape[0]
    outgoing, table = pl.pallas_call(
        front_kernel,
        out_shape=[jax.ShapeDtypeStruct((slots, raw), BF), jax.ShapeDtypeStruct((tok, slots), BF)],
        in_specs=[vmem] * 5,
        out_specs=[vmem] * 2,
        scratch_shapes=[pltpu.VMEM((padded.size // chans, 3 * chans), BF)],
        compiler_params=params,
    )(padded, conv_weight.reshape(3, 3, 3 * chans, chans), jnp.tile(latent_weight, (1, 8)), context, routes)

    arrived = lax.all_to_all(outgoing.reshape(experts, capacity, raw), SOURCES, split_axis=0, concat_axis=0, tiled=True)
    mine = arrived.reshape(slots, raw)
    theirs = lax.ppermute(mine, "x", XOR3)
    across, mine = lax.optimization_barrier((across, mine))
    corner = lax.ppermute(across, "c", SWAP)
    weights = (held, beside, across, corner)
    place = jnp.stack([lax.axis_index(axis) for axis in FRAME]).astype(jnp.int32)

    def expert(block):
        return pl.pallas_call(
            expert_kernel,
            out_shape=jax.ShapeDtypeStruct((slots, width), BF),
            in_specs=[smem] + [vmem] * 6,
            out_specs=vmem,
            scratch_shapes=[pltpu.VMEM((16, embed_weight.shape[1], 128), BF)],
            compiler_params=params,
        )(place, block, router_weight[:, :, 0], *weights)

    back = lax.ppermute(expert(theirs), "x", XOR3)
    own = expert(mine)
    summed = (back.astype(F32) + own.astype(F32)).astype(BF).reshape(experts, capacity, width)
    homeward = lax.all_to_all(summed, SOURCES, split_axis=0, concat_axis=0, tiled=True)
    return dot(table, homeward.reshape(slots, width)).astype(BF)


def solution(mesh):
    fine = Mesh(mesh.devices.reshape(SIZES), NAMES)
    return jax.shard_map(
        local,
        mesh=fine,
        in_specs=(
            P(FRAME, EXPERT, None, None),
            P(),
            P(),
            P(None, FRAME),
            P((*FRAME, *EXPERT), None),
            P(None, None, EXPERT),
            P(EXPERT, None, FRAME),
            P(EXPERT, None, FRAME),
            P(EXPERT, FRAME, None),
            P((*FRAME, *EXPERT), None),
        ),
        out_specs=P((*FRAME, *EXPERT), None),
        check_vma=False,
    )
```

```python
import jax
import jax.numpy as jnp
from jax import lax
from jax.experimental import pallas as pl
from jax.experimental.pallas import tpu as pltpu
from jax.sharding import Mesh, PartitionSpec as P

FRAME = ("yh", "x", "c")
EXPERT = ("yl", "z")
SOURCES = ("yh", "yl", "z")
SIZES = (2, 4, 2, 4, 8)
NAMES = ("yh", "x", "c", "yl", "z")
BF = jnp.bfloat16
F32 = jnp.float32
SWAP = [(0, 1), (1, 0)]
VMEM_BYTES = 16 * 1024 * 1024
PACK_BYTES = 66_400_000


def dot(a, b, dims=((1,), (0,))):
    return lax.dot_general(a, b, (dims, ((), ())), preferred_element_type=F32)


def shifted(value, axes, step):
    count = lax.axis_size(axes)
    pairs = [(i, i + step) for i in range(count) if 0 <= i + step < count]
    return lax.ppermute(value, axes, pairs)


def ring(value, step):
    return lax.ppermute(value, "x", [(i, (i - step) % 4) for i in range(4)])


def silu(value):
    return value / (1.0 + jnp.exp(-value))


def lay_beside(out_ref, at, *refs):
    tall = len(refs) * refs[0].shape[0] * 128 // 1536
    lane = 0
    for ref in refs:
        for row in range(0, ref.shape[0], tall):
            out_ref[at : at + tall, lane : lane + 128] = ref[row : row + tall]
            lane += 128


def pack_kernel(
    gate_ref, up_ref, down_ref, own_ref, other_ref, first_ref, second_ref, first_held, second_held, sems
):
    share = down_ref.shape[0]
    half, part = share // 2, 3 * share // 2
    copies = [
        pltpu.make_async_copy(gate_ref, first_held.at[pl.ds(0, share)], sems.at[0]),
        pltpu.make_async_copy(up_ref.at[pl.ds(0, half)], first_held.at[pl.ds(share, half)], sems.at[1]),
        pltpu.make_async_copy(up_ref.at[pl.ds(half, half)], second_held.at[pl.ds(0, half)], sems.at[2]),
        pltpu.make_async_copy(down_ref, second_held.at[pl.ds(half, share)], sems.at[3]),
    ]
    for copy in copies:
        copy.start()
    lay_beside(first_held, part, own_ref, other_ref)
    for copy in copies:
        copy.wait()
    copies = [
        pltpu.make_async_copy(first_held, first_ref, sems.at[4]),
        pltpu.make_async_copy(second_held, second_ref, sems.at[5]),
    ]
    for copy in copies:
        copy.start()
    for copy in copies:
        copy.wait()


def front_kernel(tall_ref, conv_ref, latent_ref, context_ref, routes_ref, out_ref, table_ref, wide_ref):
    frames, rows, cols, chans = tall_ref.shape
    tok, width = context_ref.shape
    slots = table_ref.shape[1]

    flat = tall_ref[...].reshape(frames * rows * cols, chans).astype(F32)
    column = lax.broadcasted_iota(jnp.int32, flat.shape, 0) % cols
    wide_ref[:, :chans] = jnp.where(column == 0, 0.0, pltpu.roll(flat, 1, 0)).astype(BF)
    wide_ref[:, chans : 2 * chans] = flat.astype(BF)
    wide_ref[:, 2 * chans :] = jnp.where(column == cols - 1, 0.0, pltpu.roll(flat, flat.shape[0] - 1, 0)).astype(BF)

    size = (rows - 2) * cols
    out_row = lax.broadcasted_iota(jnp.int32, (size, size), 0)
    kind, token = out_row // (size // 4), out_row % (size // 4)
    source = (token // (cols // 2) * 2 + kind // 2) * cols + token % (cols // 2) * 2 + kind % 2
    sort = (source == lax.broadcasted_iota(jnp.int32, (size, size), 1)).astype(BF)
    lat = latent_ref.shape[1] // 8
    lane = lax.broadcasted_iota(jnp.int32, latent_ref.shape, 1) // lat
    patches = jnp.zeros((tok, 8 * lat), F32)
    for frame in range(frames - 2):
        mixed = jnp.zeros((size, chans), F32)
        for a in range(3):
            for b in range(3):
                at = ((frame + a) * rows + b) * cols
                mixed += dot(wide_ref[at : at + size], conv_ref[a, b])
        video = tall_ref[frame + 2, 1 : rows - 1].reshape(size, chans).astype(F32)
        feature = (video + silu(mixed)).astype(BF)
        feature = dot(sort, feature).astype(BF)
        for part in range(4):
            weight = jnp.where(lane == frame * 4 + part, latent_ref[...], jnp.zeros((), BF))
            patches += dot(feature[part * tok : (part + 1) * tok], weight)
    patches = patches.astype(BF)

    slot = lax.broadcasted_iota(jnp.int32, (tok, slots), 1)
    chosen = (routes_ref[:, :1] == slot // 2) | (routes_ref[:, 1:] == slot // 2)
    order = [lax.broadcasted_iota(jnp.int32, (tok, tok), axis) for axis in (0, 1)]
    before = dot((order[0] > order[1]).astype(BF), chosen.astype(BF))
    table = (chosen & (before == (slot % 2).astype(F32))).astype(BF)
    table_ref[...] = table
    out_ref[:, :width] = dot(table, context_ref[...], ((0,), (0,))).astype(BF)
    out_ref[:, width:] = dot(table, patches, ((0,), (0,))).astype(BF)


def swap_kernel(rows_ref, own_ref, other_ref, a0_ref, a1_ref, a2_ref, out_ref, held_ref, sems):
    slots, (_, tall, width) = rows_ref.shape[0], held_ref.shape
    part = a0_ref.shape[0] - tall
    copies = [
        pltpu.make_async_copy(ref.at[pl.ds(part, tall)], held_ref.at[i], sems.at[i])
        for i, ref in enumerate((a0_ref, a1_ref, a2_ref))
    ]
    for copy in copies:
        copy.start()
    out_ref[:slots] = rows_ref[...]
    out_ref[slots:, width:] = jnp.zeros((out_ref.shape[0] - slots, out_ref.shape[1] - width), BF)
    lay_beside(out_ref, slots + 3 * tall, own_ref, other_ref)
    for i, copy in enumerate(copies):
        copy.wait()
        out_ref[slots + i * tall : slots + (i + 1) * tall, :width] = held_ref[i]


def near_kernel(
    at_ref,
    mine_ref,
    theirs_ref,
    router_ref,
    a0_ref,
    b0_ref,
    a1_ref,
    b1_ref,
    a2_ref,
    b2_ref,
    tokens_ref,
    score_ref,
    total_ref,
    held_ref,
    embed_ref,
    sems,
):
    yh, x, c = at_ref[0], at_ref[1], at_ref[2]
    rows, width = tokens_ref.shape[0] // 2, total_ref.shape[1]
    part = b0_ref.shape[0]
    share = part * 2 // 3
    copies = [
        pltpu.make_async_copy(ref.at[pl.ds(0, part)], held_ref.at[i // 2, pl.ds(i % 2 * part, part)], sems.at[i])
        for i, ref in enumerate((a0_ref, b0_ref, a1_ref, b1_ref, a2_ref, b2_ref))
    ]
    for copy in copies:
        copy.start()
    tall = (mine_ref.shape[0] - rows) // 4
    tiles = embed_ref.shape[1] // tall
    for core, ref in enumerate((mine_ref, theirs_ref)):
        for i, turn in enumerate((0, 3, 1, 2)):
            for j in range(2 * tiles):
                shard = (yh ^ j // tiles) * 8 + lax.rem(x + turn, 4) * 2 + (c ^ core)
                at = rows + i * tall
                embed_ref[shard, j % tiles * tall : (j % tiles + 1) * tall] = ref[at : at + tall, j * 128 : (j + 1) * 128]
    embed = embed_ref[...].reshape(width, 128)
    router = jnp.where(yh == 0, router_ref[:1], router_ref[1:]).astype(F32)
    for half, ref in enumerate((theirs_ref, mine_ref)):
        embedded = dot(ref[:rows, width:], embed, ((1,), (1,))).astype(BF)
        total = embedded.astype(F32) + ref[:rows, :width].astype(F32)
        meansq = jnp.mean(total * total, axis=1, keepdims=True)
        tokens = (total * lax.rsqrt(meansq + 1e-06)).astype(BF)
        logit = jnp.sum(tokens.astype(F32) * router, axis=1, keepdims=True)
        at = slice(half * rows, (half + 1) * rows)
        tokens_ref[at] = tokens
        score_ref[at] = 1.0 / (1.0 + jnp.exp(-logit))
    hidden = []
    for i in range(3):
        copies[2 * i].wait()
        copies[2 * i + 1].wait()
        both = dot(tokens_ref[...], held_ref[i, : 2 * share], ((1,), (1,)))
        hidden.append((silu(both[:, :share]) * both[:, share:]).astype(BF))
    hidden = jnp.concatenate(hidden, axis=1)
    tile = 512
    for at in range(0, width, tile):
        down = jnp.concatenate([held_ref[i, 2 * share :, at : at + tile] for i in range(3)], axis=0)
        total_ref[:, at : at + tile] = dot(hidden, down)


def last_kernel(tokens_ref, score_ref, total_ref, w0_ref, w1_ref, other_ref, own_ref, held_ref, sems):
    rows, width = other_ref.shape
    part, share = w1_ref.shape[0], held_ref.shape[0] // 3
    copies = [
        pltpu.make_async_copy(ref.at[pl.ds(0, part)], held_ref.at[pl.ds(i * part, part)], sems.at[i])
        for i, ref in enumerate((w0_ref, w1_ref))
    ]
    for copy in copies:
        copy.start()
    for copy in copies:
        copy.wait()
    both = dot(tokens_ref[...], held_ref[: 2 * share], ((1,), (1,)))
    hidden = (silu(both[:, :share]) * both[:, share:]).astype(BF)
    tile = 512
    for at in range(0, width, tile):
        cut = slice(at, at + tile)
        total = total_ref[:, cut] + dot(hidden, held_ref[2 * share :, cut])
        total = (total * score_ref[...]).astype(BF)
        other_ref[:, cut] = total[:rows]
        own_ref[:, cut] = total[rows:]


def local(
    video,
    conv_weight,
    latent_weight,
    embed_weight,
    context,
    router_weight,
    gate_weight,
    up_weight,
    down_weight,
    routes,
):
    rows, cols = video.shape[1:3]
    tok, width = context.shape
    experts, capacity = 64, 2
    slots = experts * capacity
    share = down_weight.shape[1]
    hbm = pl.BlockSpec(memory_space=pltpu.HBM)
    vmem = pl.BlockSpec(memory_space=pltpu.VMEM)
    smem = pl.BlockSpec(memory_space=pltpu.SMEM)
    params = pltpu.CompilerParams(vmem_limit_bytes=VMEM_BYTES)

    past = shifted(video, FRAME, 1)
    shard = embed_weight.T
    paired = lax.ppermute(shard, "yh", SWAP)
    opposite = ring(shard, 2)
    crossed = lax.ppermute(shard, ("yh", "x"), [(i, (i + 4) % 8 // 4 * 4 + (i + 2) % 4) for i in range(8)])
    part = 3 * share // 2
    tall = 2 * shard.shape[0] * shard.shape[1] // width
    first, second = pl.pallas_call(
        pack_kernel,
        out_shape=[jax.ShapeDtypeStruct((part + tall, width), BF), jax.ShapeDtypeStruct((part, width), BF)],
        in_specs=[hbm] * 3 + [vmem] * 2,
        out_specs=[hbm] * 2,
        scratch_shapes=[
            pltpu.VMEM((part + tall, width), BF),
            pltpu.VMEM((part, width), BF),
            pltpu.SemaphoreType.DMA((6,)),
        ],
        compiler_params=pltpu.CompilerParams(vmem_limit_bytes=PACK_BYTES),
    )(gate_weight[0].T, up_weight[0].T, down_weight[0], shard, paired)
    first, second, past, opposite, crossed = lax.optimization_barrier((first, second, past, opposite, crossed))
    first_behind, second_ahead = ring(first, -1), ring(second, 1)
    first_ahead, second_behind = ring(first, 1), ring(second, -1)
    first_opposite, second_opposite = ring(first_behind, -1), ring(second_ahead, 1)

    stacked = jnp.concatenate([past, video], axis=0)
    above = shifted(stacked[:, rows - 1 :], EXPERT, 1)
    below = shifted(stacked[:, :1], EXPERT, -1)
    padded = jnp.concatenate([above, stacked, below], axis=1)
    chans = video.shape[3]
    raw = width + embed_weight.shape[0]
    outgoing, table = pl.pallas_call(
        front_kernel,
        out_shape=[jax.ShapeDtypeStruct((slots, raw), BF), jax.ShapeDtypeStruct((tok, slots), BF)],
        in_specs=[vmem] * 5,
        out_specs=[vmem] * 2,
        scratch_shapes=[pltpu.VMEM((padded.size // chans, 3 * chans), BF)],
        compiler_params=params,
    )(padded, conv_weight.reshape(3, 3, 3 * chans, chans), jnp.tile(latent_weight, (1, 8)), context, routes)

    arrived = lax.all_to_all(outgoing.reshape(experts, capacity, raw), SOURCES, split_axis=0, concat_axis=0, tiled=True)
    arrived, first_ahead, second_behind = lax.optimization_barrier((arrived, first_ahead, second_behind))
    mine = pl.pallas_call(
        swap_kernel,
        out_shape=jax.ShapeDtypeStruct((slots + 4 * tall, raw), BF),
        in_specs=[vmem] * 3 + [hbm] * 3,
        out_specs=vmem,
        scratch_shapes=[pltpu.VMEM((3, tall, width), BF), pltpu.SemaphoreType.DMA((3,))],
        compiler_params=params,
    )(arrived.reshape(slots, raw), opposite, crossed, first, first_behind, first_ahead)
    theirs = lax.ppermute(mine, "c", SWAP)
    place = jnp.stack([lax.axis_index(axis) for axis in FRAME]).astype(jnp.int32)
    tokens, score, total = pl.pallas_call(
        near_kernel,
        out_shape=[
            jax.ShapeDtypeStruct((2 * slots, width), BF),
            jax.ShapeDtypeStruct((2 * slots, 1), F32),
            jax.ShapeDtypeStruct((2 * slots, width), F32),
        ],
        in_specs=[smem] + [vmem] * 3 + [hbm] * 6,
        out_specs=[vmem] * 3,
        scratch_shapes=[
            pltpu.VMEM((3, 3 * share, width), BF),
            pltpu.VMEM((16, embed_weight.shape[1], 128), BF),
            pltpu.SemaphoreType.DMA((6,)),
        ],
        compiler_params=params,
    )(place, mine, theirs, router_weight[:, :, 0], first, second, first_behind, second_behind, first_ahead, second_ahead)
    other, own = pl.pallas_call(
        last_kernel,
        out_shape=[jax.ShapeDtypeStruct((slots, width), BF)] * 2,
        in_specs=[vmem] * 3 + [hbm] * 2,
        out_specs=[vmem] * 2,
        scratch_shapes=[pltpu.VMEM((3 * share, width), BF), pltpu.SemaphoreType.DMA((2,))],
        compiler_params=params,
    )(tokens, score, total, first_opposite, second_opposite)
    back = lax.ppermute(other, "c", SWAP)
    summed = (back.astype(F32) + own.astype(F32)).astype(BF).reshape(experts, capacity, width)
    homeward = lax.all_to_all(summed, SOURCES, split_axis=0, concat_axis=0, tiled=True)
    return dot(table, homeward.reshape(slots, width)).astype(BF)


def solution(mesh):
    fine = Mesh(mesh.devices.reshape(SIZES), NAMES)
    return jax.shard_map(
        local,
        mesh=fine,
        in_specs=(
            P(FRAME, EXPERT, None, None),
            P(),
            P(),
            P(None, FRAME),
            P((*FRAME, *EXPERT), None),
            P(None, None, EXPERT),
            P(EXPERT, None, FRAME),
            P(EXPERT, None, FRAME),
            P(EXPERT, FRAME, None),
            P((*FRAME, *EXPERT), None),
        ),
        out_specs=P((*FRAME, *EXPERT), None),
        check_vma=False,
    )
```

```python
import jax
import jax.numpy as jnp
from jax import lax
from jax.experimental import pallas as pl
from jax.experimental.pallas import tpu as pltpu
from jax.sharding import Mesh, PartitionSpec as P

FRAME = ("yh", "x", "c")
EXPERT = ("yl", "z")
SOURCES = ("yh", "yl", "z")
SIZES = (2, 4, 2, 4, 8)
NAMES = ("yh", "x", "c", "yl", "z")
BF = jnp.bfloat16
F32 = jnp.float32
SWAP = [(0, 1), (1, 0)]
VMEM_BYTES = 16 * 1024 * 1024
PACK_BYTES = 66_400_000
SWAP_BYTES = 65_600_000
NEAR_BYTES = 62_500_000


def dot(a, b, dims=((1,), (0,))):
    return lax.dot_general(a, b, (dims, ((), ())), preferred_element_type=F32)


def shifted(value, axes, step):
    count = lax.axis_size(axes)
    pairs = [(i, i + step) for i in range(count) if 0 <= i + step < count]
    return lax.ppermute(value, axes, pairs)


def ring(value, step):
    return lax.ppermute(value, "x", [(i, (i - step) % 4) for i in range(4)])


def silu(value):
    return value / (1.0 + jnp.exp(-value))


def lay_beside(out_ref, at, *refs):
    tall = len(refs) * refs[0].shape[0] * 128 // 1536
    lane = 0
    for ref in refs:
        for row in range(0, ref.shape[0], tall):
            out_ref[at : at + tall, lane : lane + 128] = ref[row : row + tall]
            lane += 128


def pack_kernel(gate_ref, up_ref, down_ref, own_ref, other_ref, out_ref, embed_ref, held_ref, sems):
    share = down_ref.shape[0]
    copies = [
        pltpu.make_async_copy(ref, held_ref.at[pl.ds(i * share, share)], sems.at[i])
        for i, ref in enumerate((gate_ref, up_ref, down_ref))
    ]
    for copy in copies:
        copy.start()
    lay_beside(embed_ref, 0, own_ref, other_ref)
    held_ref[3 * share :] = embed_ref[...]
    for copy in copies:
        copy.wait()
    copy = pltpu.make_async_copy(held_ref, out_ref, sems.at[3])
    copy.start()
    copy.wait()


def halves_kernel(behind_ref, ahead_ref, first_ref, second_ref, first_held, second_held, sems):
    part = first_ref.shape[0]
    copies = [
        pltpu.make_async_copy(behind_ref.at[pl.ds(0, part)], first_held, sems.at[0]),
        pltpu.make_async_copy(ahead_ref.at[pl.ds(part, part)], second_held, sems.at[1]),
    ]
    back = [
        pltpu.make_async_copy(first_held, first_ref, sems.at[2]),
        pltpu.make_async_copy(second_held, second_ref, sems.at[3]),
    ]
    for copy in copies:
        copy.start()
    for copy, then in zip(copies, back):
        copy.wait()
        then.start()
    for copy in back:
        copy.wait()


def front_kernel(tall_ref, conv_ref, latent_ref, context_ref, routes_ref, out_ref, table_ref, wide_ref):
    frames, rows, cols, chans = tall_ref.shape
    tok, width = context_ref.shape
    slots = table_ref.shape[1]

    flat = tall_ref[...].reshape(frames * rows * cols, chans).astype(F32)
    column = lax.broadcasted_iota(jnp.int32, flat.shape, 0) % cols
    wide_ref[:, :chans] = jnp.where(column == 0, 0.0, pltpu.roll(flat, 1, 0)).astype(BF)
    wide_ref[:, chans : 2 * chans] = flat.astype(BF)
    wide_ref[:, 2 * chans :] = jnp.where(column == cols - 1, 0.0, pltpu.roll(flat, flat.shape[0] - 1, 0)).astype(BF)

    size = (rows - 2) * cols
    out_row = lax.broadcasted_iota(jnp.int32, (size, size), 0)
    kind, token = out_row // (size // 4), out_row % (size // 4)
    source = (token // (cols // 2) * 2 + kind // 2) * cols + token % (cols // 2) * 2 + kind % 2
    sort = (source == lax.broadcasted_iota(jnp.int32, (size, size), 1)).astype(BF)
    lat = latent_ref.shape[1] // 8
    lane = lax.broadcasted_iota(jnp.int32, latent_ref.shape, 1) // lat
    patches = jnp.zeros((tok, 8 * lat), F32)
    for frame in range(frames - 2):
        mixed = jnp.zeros((size, chans), F32)
        for a in range(3):
            for b in range(3):
                at = ((frame + a) * rows + b) * cols
                mixed += dot(wide_ref[at : at + size], conv_ref[a, b])
        video = tall_ref[frame + 2, 1 : rows - 1].reshape(size, chans).astype(F32)
        feature = (video + silu(mixed)).astype(BF)
        feature = dot(sort, feature).astype(BF)
        for part in range(4):
            weight = jnp.where(lane == frame * 4 + part, latent_ref[...], jnp.zeros((), BF))
            patches += dot(feature[part * tok : (part + 1) * tok], weight)
    patches = patches.astype(BF)

    slot = lax.broadcasted_iota(jnp.int32, (tok, slots), 1)
    chosen = (routes_ref[:, :1] == slot // 2) | (routes_ref[:, 1:] == slot // 2)
    order = [lax.broadcasted_iota(jnp.int32, (tok, tok), axis) for axis in (0, 1)]
    before = dot((order[0] > order[1]).astype(BF), chosen.astype(BF))
    table = (chosen & (before == (slot % 2).astype(F32))).astype(BF)
    table_ref[...] = table
    out_ref[:, :width] = dot(table, context_ref[...], ((0,), (0,))).astype(BF)
    out_ref[:, width:] = dot(table, patches, ((0,), (0,))).astype(BF)


def swap_kernel(rows_ref, embed_ref, a0_ref, a1_ref, a2_ref, out_ref, held_ref, sems):
    slots, (_, tall, width) = rows_ref.shape[0], held_ref.shape
    part = a0_ref.shape[0] - tall
    copies = [
        pltpu.make_async_copy(ref.at[pl.ds(part, tall)], held_ref.at[i], sems.at[i])
        for i, ref in enumerate((a0_ref, a1_ref, a2_ref))
    ]
    for copy in copies:
        copy.start()
    out_ref[:slots] = rows_ref[...]
    out_ref[slots:, width:] = jnp.zeros((out_ref.shape[0] - slots, out_ref.shape[1] - width), BF)
    out_ref[slots + 3 * tall :, :width] = embed_ref[...]
    for i, copy in enumerate(copies):
        copy.wait()
        out_ref[slots + i * tall : slots + (i + 1) * tall, :width] = held_ref[i]


def near_kernel(
    at_ref,
    mine_ref,
    theirs_ref,
    router_ref,
    w0_ref,
    w1_ref,
    w2_ref,
    tokens_ref,
    score_ref,
    total_ref,
    held_ref,
    embed_ref,
    sems,
):
    yh, x, c = at_ref[0], at_ref[1], at_ref[2]
    rows, width = tokens_ref.shape[0] // 2, total_ref.shape[1]
    share = held_ref.shape[1] // 3
    copies = [
        pltpu.make_async_copy(ref.at[pl.ds(0, 3 * share)], held_ref.at[i], sems.at[i])
        for i, ref in enumerate((w0_ref, w1_ref, w2_ref))
    ]
    for copy in copies:
        copy.start()
    tall = (mine_ref.shape[0] - rows) // 4
    tiles = embed_ref.shape[1] // tall
    for core, ref in enumerate((mine_ref, theirs_ref)):
        for i, turn in enumerate((0, 3, 1, 2)):
            for j in range(2 * tiles):
                shard = (yh ^ j // tiles) * 8 + lax.rem(x + turn, 4) * 2 + (c ^ core)
                at = rows + i * tall
                embed_ref[shard, j % tiles * tall : (j % tiles + 1) * tall] = ref[at : at + tall, j * 128 : (j + 1) * 128]
    embed = embed_ref[...].reshape(width, 128)
    router = jnp.where(yh == 0, router_ref[:1], router_ref[1:]).astype(F32)
    for half, ref in enumerate((theirs_ref, mine_ref)):
        embedded = dot(ref[:rows, width:], embed, ((1,), (1,))).astype(BF)
        total = embedded.astype(F32) + ref[:rows, :width].astype(F32)
        meansq = jnp.mean(total * total, axis=1, keepdims=True)
        tokens = (total * lax.rsqrt(meansq + 1e-06)).astype(BF)
        logit = jnp.sum(tokens.astype(F32) * router, axis=1, keepdims=True)
        at = slice(half * rows, (half + 1) * rows)
        tokens_ref[at] = tokens
        score_ref[at] = 1.0 / (1.0 + jnp.exp(-logit))
    hidden = []
    for i, copy in enumerate(copies):
        copy.wait()
        both = dot(tokens_ref[...], held_ref[i, : 2 * share], ((1,), (1,)))
        hidden.append((silu(both[:, :share]) * both[:, share:]).astype(BF))
    hidden = jnp.concatenate(hidden, axis=1)
    tile = 512
    for at in range(0, width, tile):
        down = jnp.concatenate([held_ref[i, 2 * share :, at : at + tile] for i in range(3)], axis=0)
        total_ref[:, at : at + tile] = dot(hidden, down)


def last_kernel(tokens_ref, score_ref, total_ref, w0_ref, w1_ref, other_ref, own_ref, held_ref, sems):
    rows, width = other_ref.shape
    part, share = w0_ref.shape[0], held_ref.shape[0] // 3
    copies = [
        pltpu.make_async_copy(ref, held_ref.at[pl.ds(i * part, part)], sems.at[i])
        for i, ref in enumerate((w0_ref, w1_ref))
    ]
    for copy in copies:
        copy.start()
    for copy in copies:
        copy.wait()
    both = dot(tokens_ref[...], held_ref[: 2 * share], ((1,), (1,)))
    hidden = (silu(both[:, :share]) * both[:, share:]).astype(BF)
    tile = 512
    for at in range(0, width, tile):
        cut = slice(at, at + tile)
        total = total_ref[:, cut] + dot(hidden, held_ref[2 * share :, cut])
        total = (total * score_ref[...]).astype(BF)
        other_ref[:, cut] = total[:rows]
        own_ref[:, cut] = total[rows:]


def local(
    video,
    conv_weight,
    latent_weight,
    embed_weight,
    context,
    router_weight,
    gate_weight,
    up_weight,
    down_weight,
    routes,
):
    rows, cols = video.shape[1:3]
    tok, width = context.shape
    experts, capacity = 64, 2
    slots = experts * capacity
    share = down_weight.shape[1]
    hbm = pl.BlockSpec(memory_space=pltpu.HBM)
    vmem = pl.BlockSpec(memory_space=pltpu.VMEM)
    smem = pl.BlockSpec(memory_space=pltpu.SMEM)
    params = pltpu.CompilerParams(vmem_limit_bytes=VMEM_BYTES)

    past = shifted(video, FRAME, 1)
    shard = embed_weight.T
    paired = lax.ppermute(shard, "yh", SWAP)
    part = 3 * share // 2
    tall = 2 * shard.shape[0] * shard.shape[1] // width
    held, embed = pl.pallas_call(
        pack_kernel,
        out_shape=[jax.ShapeDtypeStruct((3 * share + tall, width), BF), jax.ShapeDtypeStruct((tall, width), BF)],
        in_specs=[hbm] * 3 + [vmem] * 2,
        out_specs=[hbm, vmem],
        scratch_shapes=[pltpu.VMEM((3 * share + tall, width), BF), pltpu.SemaphoreType.DMA((4,))],
        compiler_params=pltpu.CompilerParams(vmem_limit_bytes=PACK_BYTES),
    )(gate_weight[0].T, up_weight[0].T, down_weight[0], shard, paired)
    held, embed, past = lax.optimization_barrier((held, embed, past))
    behind, ahead = ring(held, -1), ring(held, 1)
    opposite = ring(embed, 2)
    first, second = pl.pallas_call(
        halves_kernel,
        out_shape=[jax.ShapeDtypeStruct((part, width), BF)] * 2,
        in_specs=[hbm] * 2,
        out_specs=[hbm] * 2,
        scratch_shapes=[pltpu.VMEM((part, width), BF)] * 2 + [pltpu.SemaphoreType.DMA((4,))],
        compiler_params=params,
    )(behind, ahead)
    first, second, opposite = lax.optimization_barrier((first, second, opposite))
    first, second = ring(first, -1), ring(second, 1)

    stacked = jnp.concatenate([past, video], axis=0)
    above = shifted(stacked[:, rows - 1 :], EXPERT, 1)
    below = shifted(stacked[:, :1], EXPERT, -1)
    padded = jnp.concatenate([above, stacked, below], axis=1)
    chans = video.shape[3]
    raw = width + embed_weight.shape[0]
    outgoing, table = pl.pallas_call(
        front_kernel,
        out_shape=[jax.ShapeDtypeStruct((slots, raw), BF), jax.ShapeDtypeStruct((tok, slots), BF)],
        in_specs=[vmem] * 5,
        out_specs=[vmem] * 2,
        scratch_shapes=[pltpu.VMEM((padded.size // chans, 3 * chans), BF)],
        compiler_params=params,
    )(padded, conv_weight.reshape(3, 3, 3 * chans, chans), jnp.tile(latent_weight, (1, 8)), context, routes)

    arrived = lax.all_to_all(outgoing.reshape(experts, capacity, raw), SOURCES, split_axis=0, concat_axis=0, tiled=True)
    mine = pl.pallas_call(
        swap_kernel,
        out_shape=jax.ShapeDtypeStruct((slots + 4 * tall, raw), BF),
        in_specs=[vmem] * 2 + [hbm] * 3,
        out_specs=vmem,
        scratch_shapes=[pltpu.VMEM((3, tall, width), BF), pltpu.SemaphoreType.DMA((3,))],
        compiler_params=pltpu.CompilerParams(vmem_limit_bytes=SWAP_BYTES),
    )(arrived.reshape(slots, raw), opposite, held, behind, ahead)
    theirs = lax.ppermute(mine, "c", SWAP)
    place = jnp.stack([lax.axis_index(axis) for axis in FRAME]).astype(jnp.int32)
    tokens, score, total = pl.pallas_call(
        near_kernel,
        out_shape=[
            jax.ShapeDtypeStruct((2 * slots, width), BF),
            jax.ShapeDtypeStruct((2 * slots, 1), F32),
            jax.ShapeDtypeStruct((2 * slots, width), F32),
        ],
        in_specs=[smem] + [vmem] * 3 + [hbm] * 3,
        out_specs=[vmem] * 3,
        scratch_shapes=[
            pltpu.VMEM((3, 3 * share, width), BF),
            pltpu.VMEM((16, embed_weight.shape[1], 128), BF),
            pltpu.SemaphoreType.DMA((3,)),
        ],
        compiler_params=pltpu.CompilerParams(vmem_limit_bytes=NEAR_BYTES),
    )(place, mine, theirs, router_weight[:, :, 0], held, behind, ahead)
    other, own = pl.pallas_call(
        last_kernel,
        out_shape=[jax.ShapeDtypeStruct((slots, width), BF)] * 2,
        in_specs=[vmem] * 3 + [hbm] * 2,
        out_specs=[vmem] * 2,
        scratch_shapes=[pltpu.VMEM((3 * share, width), BF), pltpu.SemaphoreType.DMA((2,))],
        compiler_params=params,
    )(tokens, score, total, first, second)
    back = lax.ppermute(other, "c", SWAP)
    summed = (back.astype(F32) + own.astype(F32)).astype(BF).reshape(experts, capacity, width)
    homeward = lax.all_to_all(summed, SOURCES, split_axis=0, concat_axis=0, tiled=True)
    return dot(table, homeward.reshape(slots, width)).astype(BF)


def solution(mesh):
    fine = Mesh(mesh.devices.reshape(SIZES), NAMES)
    return jax.shard_map(
        local,
        mesh=fine,
        in_specs=(
            P(FRAME, EXPERT, None, None),
            P(),
            P(),
            P(None, FRAME),
            P((*FRAME, *EXPERT), None),
            P(None, None, EXPERT),
            P(EXPERT, None, FRAME),
            P(EXPERT, None, FRAME),
            P(EXPERT, FRAME, None),
            P((*FRAME, *EXPERT), None),
        ),
        out_specs=P((*FRAME, *EXPERT), None),
        check_vma=False,
    )
```

```python
import jax
import jax.numpy as jnp
from jax import lax
from jax.experimental import pallas as pl
from jax.experimental.pallas import tpu as pltpu
from jax.sharding import Mesh, PartitionSpec as P

FRAME = ("yh", "x", "c")
EXPERT = ("yl", "z")
SOURCES = ("yh", "yl", "z")
SIZES = (2, 4, 2, 4, 8)
NAMES = ("yh", "x", "c", "yl", "z")
BF = jnp.bfloat16
F32 = jnp.float32
SWAP = [(0, 1), (1, 0)]
VMEM_BYTES = 16 * 1024 * 1024
PACK_BYTES = 66_400_000


def dot(a, b, dims=((1,), (0,))):
    return lax.dot_general(a, b, (dims, ((), ())), preferred_element_type=F32)


def shifted(value, axes, step):
    count = lax.axis_size(axes)
    pairs = [(i, i + step) for i in range(count) if 0 <= i + step < count]
    return lax.ppermute(value, axes, pairs)


def ring(value, step):
    return lax.ppermute(value, "x", [(i, (i - step) % 4) for i in range(4)])


def silu(value):
    return value / (1.0 + jnp.exp(-value))


def lay_beside(out_ref, at, ref, lane=0):
    tall = 16
    for i in range(ref.shape[0] // tall):
        lanes = slice(lane + i * 128, lane + (i + 1) * 128)
        out_ref[at : at + tall, lanes] = ref[i * tall : (i + 1) * tall]


def pack_kernel(gate_ref, up_ref, down_ref, shard_ref, first_ref, second_ref, first_held, second_held, sems):
    share = down_ref.shape[0]
    half, part = share // 2, 3 * share // 2
    copies = [
        pltpu.make_async_copy(gate_ref, first_held.at[pl.ds(0, share)], sems.at[0]),
        pltpu.make_async_copy(up_ref.at[pl.ds(0, half)], first_held.at[pl.ds(share, half)], sems.at[1]),
        pltpu.make_async_copy(up_ref.at[pl.ds(half, half)], second_held.at[pl.ds(0, half)], sems.at[2]),
        pltpu.make_async_copy(down_ref, second_held.at[pl.ds(half, share)], sems.at[3]),
    ]
    for copy in copies:
        copy.start()
    tall, width = first_held.shape[0] - part, first_held.shape[1]
    first_held[part:] = jnp.zeros((tall, width), BF)
    lay_beside(first_held, part, shard_ref)
    for copy in copies:
        copy.wait()
    copies = [
        pltpu.make_async_copy(first_held, first_ref, sems.at[4]),
        pltpu.make_async_copy(second_held, second_ref, sems.at[5]),
    ]
    for copy in copies:
        copy.start()
    for copy in copies:
        copy.wait()


def shards_kernel(opposite_ref, a0_ref, a1_ref, a2_ref, out_ref, held_ref, sems):
    tall, lanes = held_ref.shape[1], out_ref.shape[1]
    part = a0_ref.shape[0] - tall
    copies = [
        pltpu.make_async_copy(ref.at[pl.ds(part, tall)], held_ref.at[i], sems.at[i])
        for i, ref in enumerate((a0_ref, a1_ref, a2_ref))
    ]
    for copy in copies:
        copy.start()
    lay_beside(out_ref, 3 * tall, opposite_ref)
    for i, copy in enumerate(copies):
        copy.wait()
        out_ref[i * tall : (i + 1) * tall] = held_ref[i, :, :lanes]


def front_kernel(tall_ref, conv_ref, latent_ref, context_ref, routes_ref, out_ref, table_ref, wide_ref):
    frames, rows, cols, chans = tall_ref.shape
    tok, width = context_ref.shape
    slots = table_ref.shape[1]

    flat = tall_ref[...].reshape(frames * rows * cols, chans).astype(F32)
    column = lax.broadcasted_iota(jnp.int32, flat.shape, 0) % cols
    wide_ref[:, :chans] = jnp.where(column == 0, 0.0, pltpu.roll(flat, 1, 0)).astype(BF)
    wide_ref[:, chans : 2 * chans] = flat.astype(BF)
    wide_ref[:, 2 * chans :] = jnp.where(column == cols - 1, 0.0, pltpu.roll(flat, flat.shape[0] - 1, 0)).astype(BF)

    size = (rows - 2) * cols
    out_row = lax.broadcasted_iota(jnp.int32, (size, size), 0)
    kind, token = out_row // (size // 4), out_row % (size // 4)
    source = (token // (cols // 2) * 2 + kind // 2) * cols + token % (cols // 2) * 2 + kind % 2
    sort = (source == lax.broadcasted_iota(jnp.int32, (size, size), 1)).astype(BF)
    lat = latent_ref.shape[1] // 8
    lane = lax.broadcasted_iota(jnp.int32, latent_ref.shape, 1) // lat
    patches = jnp.zeros((tok, 8 * lat), F32)
    for frame in range(frames - 2):
        mixed = jnp.zeros((size, chans), F32)
        for a in range(3):
            for b in range(3):
                at = ((frame + a) * rows + b) * cols
                mixed += dot(wide_ref[at : at + size], conv_ref[a, b])
        video = tall_ref[frame + 2, 1 : rows - 1].reshape(size, chans).astype(F32)
        feature = (video + silu(mixed)).astype(BF)
        feature = dot(sort, feature).astype(BF)
        for part in range(4):
            weight = jnp.where(lane == frame * 4 + part, latent_ref[...], jnp.zeros((), BF))
            patches += dot(feature[part * tok : (part + 1) * tok], weight)
    patches = patches.astype(BF)

    slot = lax.broadcasted_iota(jnp.int32, (tok, slots), 1)
    chosen = (routes_ref[:, :1] == slot // 2) | (routes_ref[:, 1:] == slot // 2)
    order = [lax.broadcasted_iota(jnp.int32, (tok, tok), axis) for axis in (0, 1)]
    before = dot((order[0] > order[1]).astype(BF), chosen.astype(BF))
    table = (chosen & (before == (slot % 2).astype(F32))).astype(BF)
    table_ref[...] = table
    out_ref[:, :width] = dot(table, context_ref[...], ((0,), (0,))).astype(BF)
    out_ref[:, width:] = dot(table, patches, ((0,), (0,))).astype(BF)


def swap_kernel(rows_ref, near_ref, far_ref, out_ref):
    slots, lanes = rows_ref.shape[0], near_ref.shape[1]
    out_ref[:slots] = rows_ref[...]
    out_ref[slots:, :lanes] = near_ref[...]
    out_ref[slots:, lanes : 2 * lanes] = far_ref[...]
    out_ref[slots:, 2 * lanes :] = jnp.zeros((near_ref.shape[0], out_ref.shape[1] - 2 * lanes), BF)


def near_kernel(
    at_ref,
    mine_ref,
    theirs_ref,
    router_ref,
    a0_ref,
    b0_ref,
    a1_ref,
    b1_ref,
    a2_ref,
    b2_ref,
    tokens_ref,
    score_ref,
    total_ref,
    held_ref,
    embed_ref,
    sems,
):
    yh, x, c = at_ref[0], at_ref[1], at_ref[2]
    rows, width = tokens_ref.shape[0] // 2, total_ref.shape[1]
    part = b0_ref.shape[0]
    share = part * 2 // 3
    copies = [
        pltpu.make_async_copy(ref.at[pl.ds(0, part)], held_ref.at[i // 2, pl.ds(i % 2 * part, part)], sems.at[i])
        for i, ref in enumerate((a0_ref, b0_ref, a1_ref, b1_ref, a2_ref, b2_ref))
    ]
    for copy in copies:
        copy.start()
    tall = (mine_ref.shape[0] - rows) // 4
    tiles = embed_ref.shape[1] // tall
    for core, ref in enumerate((mine_ref, theirs_ref)):
        for i, turn in enumerate((0, 3, 1, 2)):
            for j in range(2 * tiles):
                shard = (yh ^ j // tiles) * 8 + lax.rem(x + turn, 4) * 2 + (c ^ core)
                at = rows + i * tall
                embed_ref[shard, j % tiles * tall : (j % tiles + 1) * tall] = ref[at : at + tall, j * 128 : (j + 1) * 128]
    embed = embed_ref[...].reshape(width, 128)
    router = jnp.where(yh == 0, router_ref[:1], router_ref[1:]).astype(F32)
    for half, ref in enumerate((theirs_ref, mine_ref)):
        embedded = dot(ref[:rows, width:], embed, ((1,), (1,))).astype(BF)
        total = embedded.astype(F32) + ref[:rows, :width].astype(F32)
        meansq = jnp.mean(total * total, axis=1, keepdims=True)
        tokens = (total * lax.rsqrt(meansq + 1e-06)).astype(BF)
        logit = jnp.sum(tokens.astype(F32) * router, axis=1, keepdims=True)
        at = slice(half * rows, (half + 1) * rows)
        tokens_ref[at] = tokens
        score_ref[at] = 1.0 / (1.0 + jnp.exp(-logit))
    hidden = []
    for i in range(3):
        copies[2 * i].wait()
        copies[2 * i + 1].wait()
        both = dot(tokens_ref[...], held_ref[i, : 2 * share], ((1,), (1,)))
        hidden.append((silu(both[:, :share]) * both[:, share:]).astype(BF))
    hidden = jnp.concatenate(hidden, axis=1)
    tile = 512
    for at in range(0, width, tile):
        down = jnp.concatenate([held_ref[i, 2 * share :, at : at + tile] for i in range(3)], axis=0)
        total_ref[:, at : at + tile] = dot(hidden, down)


def last_kernel(tokens_ref, score_ref, total_ref, w0_ref, w1_ref, other_ref, own_ref, held_ref, sems):
    rows, width = other_ref.shape
    part, share = w1_ref.shape[0], held_ref.shape[0] // 3
    copies = [
        pltpu.make_async_copy(ref.at[pl.ds(0, part)], held_ref.at[pl.ds(i * part, part)], sems.at[i])
        for i, ref in enumerate((w0_ref, w1_ref))
    ]
    for copy in copies:
        copy.start()
    for copy in copies:
        copy.wait()
    both = dot(tokens_ref[...], held_ref[: 2 * share], ((1,), (1,)))
    hidden = (silu(both[:, :share]) * both[:, share:]).astype(BF)
    tile = 512
    for at in range(0, width, tile):
        cut = slice(at, at + tile)
        total = total_ref[:, cut] + dot(hidden, held_ref[2 * share :, cut])
        total = (total * score_ref[...]).astype(BF)
        other_ref[:, cut] = total[:rows]
        own_ref[:, cut] = total[rows:]


def local(
    video,
    conv_weight,
    latent_weight,
    embed_weight,
    context,
    router_weight,
    gate_weight,
    up_weight,
    down_weight,
    routes,
):
    rows, cols = video.shape[1:3]
    tok, width = context.shape
    experts, capacity = 64, 2
    slots = experts * capacity
    share = down_weight.shape[1]
    hbm = pl.BlockSpec(memory_space=pltpu.HBM)
    vmem = pl.BlockSpec(memory_space=pltpu.VMEM)
    smem = pl.BlockSpec(memory_space=pltpu.SMEM)
    params = pltpu.CompilerParams(vmem_limit_bytes=VMEM_BYTES)

    past = shifted(video, FRAME, 1)
    shard = embed_weight.T
    part, tall = 3 * share // 2, 16
    first, second = pl.pallas_call(
        pack_kernel,
        out_shape=[jax.ShapeDtypeStruct((part + tall, width), BF), jax.ShapeDtypeStruct((part, width), BF)],
        in_specs=[hbm] * 3 + [vmem],
        out_specs=[hbm] * 2,
        scratch_shapes=[
            pltpu.VMEM((part + tall, width), BF),
            pltpu.VMEM((part, width), BF),
            pltpu.SemaphoreType.DMA((6,)),
        ],
        compiler_params=pltpu.CompilerParams(vmem_limit_bytes=PACK_BYTES),
    )(gate_weight[0].T, up_weight[0].T, down_weight[0], shard)
    first_behind, second_ahead = ring(first, -1), ring(second, 1)
    first_ahead, second_behind = ring(first, 1), ring(second, -1)
    opposite = ring(shard, 2)
    from_behind, from_ahead, opposite = lax.optimization_barrier((first_behind, second_ahead, opposite))
    first_opposite, second_opposite = ring(from_behind, -1), ring(from_ahead, 1)

    stacked = jnp.concatenate([past, video], axis=0)
    above = shifted(stacked[:, rows - 1 :], EXPERT, 1)
    below = shifted(stacked[:, :1], EXPERT, -1)
    padded = jnp.concatenate([above, stacked, below], axis=1)
    chans = video.shape[3]
    raw = width + embed_weight.shape[0]
    outgoing, table = pl.pallas_call(
        front_kernel,
        out_shape=[jax.ShapeDtypeStruct((slots, raw), BF), jax.ShapeDtypeStruct((tok, slots), BF)],
        in_specs=[vmem] * 5,
        out_specs=[vmem] * 2,
        scratch_shapes=[pltpu.VMEM((padded.size // chans, 3 * chans), BF)],
        compiler_params=params,
    )(padded, conv_weight.reshape(3, 3, 3 * chans, chans), jnp.tile(latent_weight, (1, 8)), context, routes)

    arrived = lax.all_to_all(outgoing.reshape(experts, capacity, raw), SOURCES, split_axis=0, concat_axis=0, tiled=True)
    lanes = shard.shape[0] // tall * 128
    shards = pl.pallas_call(
        shards_kernel,
        out_shape=jax.ShapeDtypeStruct((4 * tall, lanes), BF),
        in_specs=[vmem] + [hbm] * 3,
        out_specs=vmem,
        scratch_shapes=[pltpu.VMEM((3, tall, width), BF), pltpu.SemaphoreType.DMA((3,))],
        compiler_params=params,
    )(opposite, first, first_behind, first_ahead)
    beyond = lax.ppermute(shards, "yh", SWAP)
    arrived, beyond, second_behind = lax.optimization_barrier((arrived, beyond, second_behind))
    mine = pl.pallas_call(
        swap_kernel,
        out_shape=jax.ShapeDtypeStruct((slots + 4 * tall, raw), BF),
        in_specs=[vmem] * 3,
        out_specs=vmem,
        compiler_params=params,
    )(arrived.reshape(slots, raw), shards, beyond)
    theirs = lax.ppermute(mine, "c", SWAP)
    place = jnp.stack([lax.axis_index(axis) for axis in FRAME]).astype(jnp.int32)
    tokens, score, total = pl.pallas_call(
        near_kernel,
        out_shape=[
            jax.ShapeDtypeStruct((2 * slots, width), BF),
            jax.ShapeDtypeStruct((2 * slots, 1), F32),
            jax.ShapeDtypeStruct((2 * slots, width), F32),
        ],
        in_specs=[smem] + [vmem] * 3 + [hbm] * 6,
        out_specs=[vmem] * 3,
        scratch_shapes=[
            pltpu.VMEM((3, 3 * share, width), BF),
            pltpu.VMEM((16, embed_weight.shape[1], 128), BF),
            pltpu.SemaphoreType.DMA((6,)),
        ],
        compiler_params=params,
    )(place, mine, theirs, router_weight[:, :, 0], first, second, first_behind, second_behind, first_ahead, second_ahead)
    other, own = pl.pallas_call(
        last_kernel,
        out_shape=[jax.ShapeDtypeStruct((slots, width), BF)] * 2,
        in_specs=[vmem] * 3 + [hbm] * 2,
        out_specs=[vmem] * 2,
        scratch_shapes=[pltpu.VMEM((3 * share, width), BF), pltpu.SemaphoreType.DMA((2,))],
        compiler_params=params,
    )(tokens, score, total, first_opposite, second_opposite)
    back = lax.ppermute(other, "c", SWAP)
    summed = (back.astype(F32) + own.astype(F32)).astype(BF).reshape(experts, capacity, width)
    homeward = lax.all_to_all(summed, SOURCES, split_axis=0, concat_axis=0, tiled=True)
    return dot(table, homeward.reshape(slots, width)).astype(BF)


def solution(mesh):
    fine = Mesh(mesh.devices.reshape(SIZES), NAMES)
    return jax.shard_map(
        local,
        mesh=fine,
        in_specs=(
            P(FRAME, EXPERT, None, None),
            P(),
            P(),
            P(None, FRAME),
            P((*FRAME, *EXPERT), None),
            P(None, None, EXPERT),
            P(EXPERT, None, FRAME),
            P(EXPERT, None, FRAME),
            P(EXPERT, FRAME, None),
            P((*FRAME, *EXPERT), None),
        ),
        out_specs=P((*FRAME, *EXPERT), None),
        check_vma=False,
    )
```

```python
import jax
import jax.numpy as jnp
from jax import lax
from jax.experimental import pallas as pl
from jax.experimental.pallas import tpu as pltpu
from jax.sharding import Mesh, PartitionSpec as P

FRAME = ("yh", "x", "c")
EXPERT = ("yl", "z")
SOURCES = ("yh", "yl", "z")
SIZES = (2, 4, 2, 4, 8)
NAMES = ("yh", "x", "c", "yl", "z")
BF = jnp.bfloat16
F32 = jnp.float32
SWAP = [(0, 1), (1, 0)]
VMEM_BYTES = 16 * 1024 * 1024
PACK_BYTES = 66_400_000


def dot(a, b, dims=((1,), (0,))):
    return lax.dot_general(a, b, (dims, ((), ())), preferred_element_type=F32)


def shifted(value, axes, step):
    count = lax.axis_size(axes)
    pairs = [(i, i + step) for i in range(count) if 0 <= i + step < count]
    return lax.ppermute(value, axes, pairs)


def ring(value, step):
    return lax.ppermute(value, "x", [(i, (i - step) % 4) for i in range(4)])


def silu(value):
    return value / (1.0 + jnp.exp(-value))


def lay_beside(out_ref, at, *refs):
    tall = len(refs) * refs[0].shape[0] * 128 // 1536
    lane = 0
    for ref in refs:
        for row in range(0, ref.shape[0], tall):
            out_ref[at : at + tall, lane : lane + 128] = ref[row : row + tall]
            lane += 128


def bring(pairs, sems):
    copies = [pltpu.make_async_copy(source, target, sems.at[i]) for i, (source, target) in enumerate(pairs)]
    for copy in copies:
        copy.start()
    return copies


def pack_first_kernel(gate_ref, up_ref, out_ref, held_ref, sems):
    share, part = gate_ref.shape[0], out_ref.shape[0]
    pairs = [(gate_ref, held_ref.at[pl.ds(0, share)]), (up_ref.at[pl.ds(0, part - share)], held_ref.at[pl.ds(share, part - share)])]
    for copy in bring(pairs, sems):
        copy.wait()
    for copy in bring([(held_ref, out_ref)], sems):
        copy.wait()


def pack_second_kernel(up_ref, down_ref, own_ref, other_ref, out_ref, held_ref, sems):
    share = down_ref.shape[0]
    half = share // 2
    pairs = [(up_ref.at[pl.ds(half, half)], held_ref.at[pl.ds(0, half)]), (down_ref, held_ref.at[pl.ds(half, share)])]
    copies = bring(pairs, sems)
    lay_beside(held_ref, half + share, own_ref, other_ref)
    for copy in copies:
        copy.wait()
    for copy in bring([(held_ref, out_ref)], sems):
        copy.wait()


def front_kernel(tall_ref, conv_ref, latent_ref, context_ref, routes_ref, out_ref, table_ref, wide_ref):
    frames, rows, cols, chans = tall_ref.shape
    tok, width = context_ref.shape
    slots = table_ref.shape[1]

    flat = tall_ref[...].reshape(frames * rows * cols, chans).astype(F32)
    column = lax.broadcasted_iota(jnp.int32, flat.shape, 0) % cols
    wide_ref[:, :chans] = jnp.where(column == 0, 0.0, pltpu.roll(flat, 1, 0)).astype(BF)
    wide_ref[:, chans : 2 * chans] = flat.astype(BF)
    wide_ref[:, 2 * chans :] = jnp.where(column == cols - 1, 0.0, pltpu.roll(flat, flat.shape[0] - 1, 0)).astype(BF)

    size = (rows - 2) * cols
    out_row = lax.broadcasted_iota(jnp.int32, (size, size), 0)
    kind, token = out_row // (size // 4), out_row % (size // 4)
    source = (token // (cols // 2) * 2 + kind // 2) * cols + token % (cols // 2) * 2 + kind % 2
    sort = (source == lax.broadcasted_iota(jnp.int32, (size, size), 1)).astype(BF)
    lat = latent_ref.shape[1] // 8
    lane = lax.broadcasted_iota(jnp.int32, latent_ref.shape, 1) // lat
    patches = jnp.zeros((tok, 8 * lat), F32)
    for frame in range(frames - 2):
        mixed = jnp.zeros((size, chans), F32)
        for a in range(3):
            for b in range(3):
                at = ((frame + a) * rows + b) * cols
                mixed += dot(wide_ref[at : at + size], conv_ref[a, b])
        video = tall_ref[frame + 2, 1 : rows - 1].reshape(size, chans).astype(F32)
        feature = (video + silu(mixed)).astype(BF)
        feature = dot(sort, feature).astype(BF)
        for part in range(4):
            weight = jnp.where(lane == frame * 4 + part, latent_ref[...], jnp.zeros((), BF))
            patches += dot(feature[part * tok : (part + 1) * tok], weight)
    patches = patches.astype(BF)

    slot = lax.broadcasted_iota(jnp.int32, (tok, slots), 1)
    chosen = (routes_ref[:, :1] == slot // 2) | (routes_ref[:, 1:] == slot // 2)
    order = [lax.broadcasted_iota(jnp.int32, (tok, tok), axis) for axis in (0, 1)]
    before = dot((order[0] > order[1]).astype(BF), chosen.astype(BF))
    table = (chosen & (before == (slot % 2).astype(F32))).astype(BF)
    table_ref[...] = table
    out_ref[:, :width] = dot(table, context_ref[...], ((0,), (0,))).astype(BF)
    out_ref[:, width:] = dot(table, patches, ((0,), (0,))).astype(BF)


def swap_kernel(rows_ref, own_ref, other_ref, a0_ref, a1_ref, a2_ref, out_ref, held_ref, sems):
    slots, (_, tall, width) = rows_ref.shape[0], held_ref.shape
    part = a0_ref.shape[0] - tall
    copies = [
        pltpu.make_async_copy(ref.at[pl.ds(part, tall)], held_ref.at[i], sems.at[i])
        for i, ref in enumerate((a0_ref, a1_ref, a2_ref))
    ]
    for copy in copies:
        copy.start()
    out_ref[:slots] = rows_ref[...]
    out_ref[slots:, width:] = jnp.zeros((out_ref.shape[0] - slots, out_ref.shape[1] - width), BF)
    lay_beside(out_ref, slots + 3 * tall, own_ref, other_ref)
    for i, copy in enumerate(copies):
        copy.wait()
        out_ref[slots + i * tall : slots + (i + 1) * tall, :width] = held_ref[i]


def near_kernel(
    at_ref,
    mine_ref,
    theirs_ref,
    router_ref,
    a0_ref,
    b0_ref,
    a1_ref,
    b1_ref,
    a2_ref,
    b2_ref,
    tokens_ref,
    score_ref,
    total_ref,
    held_ref,
    embed_ref,
    sems,
):
    yh, x, c = at_ref[0], at_ref[1], at_ref[2]
    rows, width = tokens_ref.shape[0] // 2, total_ref.shape[1]
    part = a0_ref.shape[0]
    share = part * 2 // 3
    copies = [
        pltpu.make_async_copy(ref.at[pl.ds(0, part)], held_ref.at[i // 2, pl.ds(i % 2 * part, part)], sems.at[i])
        for i, ref in enumerate((a0_ref, b0_ref, a1_ref, b1_ref, a2_ref, b2_ref))
    ]
    for copy in copies:
        copy.start()
    tall = (mine_ref.shape[0] - rows) // 4
    tiles = embed_ref.shape[1] // tall
    for core, ref in enumerate((mine_ref, theirs_ref)):
        for i, turn in enumerate((0, 3, 1, 2)):
            for j in range(2 * tiles):
                shard = (yh ^ j // tiles) * 8 + lax.rem(x + turn, 4) * 2 + (c ^ core)
                at = rows + i * tall
                embed_ref[shard, j % tiles * tall : (j % tiles + 1) * tall] = ref[at : at + tall, j * 128 : (j + 1) * 128]
    embed = embed_ref[...].reshape(width, 128)
    router = jnp.where(yh == 0, router_ref[:1], router_ref[1:]).astype(F32)
    for half, ref in enumerate((theirs_ref, mine_ref)):
        embedded = dot(ref[:rows, width:], embed, ((1,), (1,))).astype(BF)
        total = embedded.astype(F32) + ref[:rows, :width].astype(F32)
        meansq = jnp.mean(total * total, axis=1, keepdims=True)
        tokens = (total * lax.rsqrt(meansq + 1e-06)).astype(BF)
        logit = jnp.sum(tokens.astype(F32) * router, axis=1, keepdims=True)
        at = slice(half * rows, (half + 1) * rows)
        tokens_ref[at] = tokens
        score_ref[at] = 1.0 / (1.0 + jnp.exp(-logit))
    hidden = []
    for i in range(3):
        copies[2 * i].wait()
        copies[2 * i + 1].wait()
        both = dot(tokens_ref[...], held_ref[i, : 2 * share], ((1,), (1,)))
        hidden.append((silu(both[:, :share]) * both[:, share:]).astype(BF))
    hidden = jnp.concatenate(hidden, axis=1)
    tile = 512
    for at in range(0, width, tile):
        down = jnp.concatenate([held_ref[i, 2 * share :, at : at + tile] for i in range(3)], axis=0)
        total_ref[:, at : at + tile] = dot(hidden, down)


def last_kernel(tokens_ref, score_ref, total_ref, w0_ref, w1_ref, other_ref, own_ref, held_ref, sems):
    rows, width = other_ref.shape
    part, share = w0_ref.shape[0], held_ref.shape[0] // 3
    copies = [
        pltpu.make_async_copy(ref.at[pl.ds(0, part)], held_ref.at[pl.ds(i * part, part)], sems.at[i])
        for i, ref in enumerate((w0_ref, w1_ref))
    ]
    for copy in copies:
        copy.start()
    for copy in copies:
        copy.wait()
    both = dot(tokens_ref[...], held_ref[: 2 * share], ((1,), (1,)))
    hidden = (silu(both[:, :share]) * both[:, share:]).astype(BF)
    tile = 512
    for at in range(0, width, tile):
        cut = slice(at, at + tile)
        total = total_ref[:, cut] + dot(hidden, held_ref[2 * share :, cut])
        total = (total * score_ref[...]).astype(BF)
        other_ref[:, cut] = total[:rows]
        own_ref[:, cut] = total[rows:]


def local(
    video,
    conv_weight,
    latent_weight,
    embed_weight,
    context,
    router_weight,
    gate_weight,
    up_weight,
    down_weight,
    routes,
):
    rows, cols = video.shape[1:3]
    tok, width = context.shape
    experts, capacity = 64, 2
    slots = experts * capacity
    share = down_weight.shape[1]
    hbm = pl.BlockSpec(memory_space=pltpu.HBM)
    vmem = pl.BlockSpec(memory_space=pltpu.VMEM)
    smem = pl.BlockSpec(memory_space=pltpu.SMEM)
    params = pltpu.CompilerParams(vmem_limit_bytes=VMEM_BYTES)

    past = shifted(video, FRAME, 1)
    shard = embed_weight.T
    paired = lax.ppermute(shard, "yh", SWAP)
    opposite = ring(shard, 2)
    crossed = lax.ppermute(shard, ("yh", "x"), [(i, (i + 4) % 8 // 4 * 4 + (i + 2) % 4) for i in range(8)])
    part = 3 * share // 2
    tall = 2 * shard.shape[0] * shard.shape[1] // width
    wide = pltpu.CompilerParams(vmem_limit_bytes=PACK_BYTES)
    gate, up, down = gate_weight[0].T, up_weight[0].T, down_weight[0]
    first = pl.pallas_call(
        pack_first_kernel,
        out_shape=jax.ShapeDtypeStruct((part, width), BF),
        in_specs=[hbm] * 2,
        out_specs=hbm,
        scratch_shapes=[pltpu.VMEM((part, width), BF), pltpu.SemaphoreType.DMA((2,))],
        compiler_params=wide,
    )(gate, up)
    second = pl.pallas_call(
        pack_second_kernel,
        out_shape=jax.ShapeDtypeStruct((part + tall, width), BF),
        in_specs=[hbm] * 2 + [vmem] * 2,
        out_specs=hbm,
        scratch_shapes=[pltpu.VMEM((part + tall, width), BF), pltpu.SemaphoreType.DMA((2,))],
        compiler_params=wide,
    )(up, down, shard, paired)
    first_behind, first_ahead = ring(first, -1), ring(first, 1)
    second, opposite, crossed = lax.optimization_barrier((second, opposite, crossed))
    second_ahead, second_behind = ring(second, 1), ring(second, -1)
    first_opposite, second_opposite = ring(first_behind, -1), ring(second_ahead, 1)

    stacked = jnp.concatenate([past, video], axis=0)
    above = shifted(stacked[:, rows - 1 :], EXPERT, 1)
    below = shifted(stacked[:, :1], EXPERT, -1)
    padded = jnp.concatenate([above, stacked, below], axis=1)
    chans = video.shape[3]
    raw = width + embed_weight.shape[0]
    outgoing, table = pl.pallas_call(
        front_kernel,
        out_shape=[jax.ShapeDtypeStruct((slots, raw), BF), jax.ShapeDtypeStruct((tok, slots), BF)],
        in_specs=[vmem] * 5,
        out_specs=[vmem] * 2,
        scratch_shapes=[pltpu.VMEM((padded.size // chans, 3 * chans), BF)],
        compiler_params=params,
    )(padded, conv_weight.reshape(3, 3, 3 * chans, chans), jnp.tile(latent_weight, (1, 8)), context, routes)

    arrived = lax.all_to_all(outgoing.reshape(experts, capacity, raw), SOURCES, split_axis=0, concat_axis=0, tiled=True)
    arrived, first_ahead, second_behind = lax.optimization_barrier((arrived, first_ahead, second_behind))
    mine = pl.pallas_call(
        swap_kernel,
        out_shape=jax.ShapeDtypeStruct((slots + 4 * tall, raw), BF),
        in_specs=[vmem] * 3 + [hbm] * 3,
        out_specs=vmem,
        scratch_shapes=[pltpu.VMEM((3, tall, width), BF), pltpu.SemaphoreType.DMA((3,))],
        compiler_params=params,
    )(arrived.reshape(slots, raw), opposite, crossed, second, second_behind, second_ahead)
    theirs = lax.ppermute(mine, "c", SWAP)
    place = jnp.stack([lax.axis_index(axis) for axis in FRAME]).astype(jnp.int32)
    tokens, score, total = pl.pallas_call(
        near_kernel,
        out_shape=[
            jax.ShapeDtypeStruct((2 * slots, width), BF),
            jax.ShapeDtypeStruct((2 * slots, 1), F32),
            jax.ShapeDtypeStruct((2 * slots, width), F32),
        ],
        in_specs=[smem] + [vmem] * 3 + [hbm] * 6,
        out_specs=[vmem] * 3,
        scratch_shapes=[
            pltpu.VMEM((3, 3 * share, width), BF),
            pltpu.VMEM((16, embed_weight.shape[1], 128), BF),
            pltpu.SemaphoreType.DMA((6,)),
        ],
        compiler_params=params,
    )(place, mine, theirs, router_weight[:, :, 0], first, second, first_behind, second_behind, first_ahead, second_ahead)
    other, own = pl.pallas_call(
        last_kernel,
        out_shape=[jax.ShapeDtypeStruct((slots, width), BF)] * 2,
        in_specs=[vmem] * 3 + [hbm] * 2,
        out_specs=[vmem] * 2,
        scratch_shapes=[pltpu.VMEM((3 * share, width), BF), pltpu.SemaphoreType.DMA((2,))],
        compiler_params=params,
    )(tokens, score, total, first_opposite, second_opposite)
    back = lax.ppermute(other, "c", SWAP)
    summed = (back.astype(F32) + own.astype(F32)).astype(BF).reshape(experts, capacity, width)
    homeward = lax.all_to_all(summed, SOURCES, split_axis=0, concat_axis=0, tiled=True)
    return dot(table, homeward.reshape(slots, width)).astype(BF)


def solution(mesh):
    fine = Mesh(mesh.devices.reshape(SIZES), NAMES)
    return jax.shard_map(
        local,
        mesh=fine,
        in_specs=(
            P(FRAME, EXPERT, None, None),
            P(),
            P(),
            P(None, FRAME),
            P((*FRAME, *EXPERT), None),
            P(None, None, EXPERT),
            P(EXPERT, None, FRAME),
            P(EXPERT, None, FRAME),
            P(EXPERT, FRAME, None),
            P((*FRAME, *EXPERT), None),
        ),
        out_specs=P((*FRAME, *EXPERT), None),
        check_vma=False,
    )
```

```python
import jax
import jax.numpy as jnp
from jax import lax
from jax.experimental import pallas as pl
from jax.experimental.pallas import tpu as pltpu
from jax.sharding import Mesh, PartitionSpec as P

FRAME = ("yh", "x", "c")
EXPERT = ("yl", "z")
SOURCES = ("yh", "yl", "z")
SIZES = (2, 4, 2, 4, 8)
NAMES = ("yh", "x", "c", "yl", "z")
BF = jnp.bfloat16
F32 = jnp.float32
SWAP = [(0, 1), (1, 0)]
VMEM_BYTES = 16 * 1024 * 1024
PACK_BYTES = 66_400_000


def dot(a, b, dims=((1,), (0,))):
    return lax.dot_general(a, b, (dims, ((), ())), preferred_element_type=F32)


def shifted(value, axes, step):
    count = lax.axis_size(axes)
    pairs = [(i, i + step) for i in range(count) if 0 <= i + step < count]
    return lax.ppermute(value, axes, pairs)


def ring(value, step):
    return lax.ppermute(value, "x", [(i, (i - step) % 4) for i in range(4)])


def silu(value):
    return value / (1.0 + jnp.exp(-value))


def lay_beside(out_ref, at, ref, lane=0):
    tall = 16
    for i in range(ref.shape[0] // tall):
        lanes = slice(lane + i * 128, lane + (i + 1) * 128)
        out_ref[at : at + tall, lanes] = ref[i * tall : (i + 1) * tall]


def pack_kernel(gate_ref, up_ref, down_ref, shard_ref, first_ref, second_ref, first_held, second_held, sems):
    share = down_ref.shape[0]
    half, part = share // 2, 3 * share // 2
    copies = [
        pltpu.make_async_copy(gate_ref, first_held.at[pl.ds(0, share)], sems.at[0]),
        pltpu.make_async_copy(up_ref.at[pl.ds(0, half)], first_held.at[pl.ds(share, half)], sems.at[1]),
        pltpu.make_async_copy(up_ref.at[pl.ds(half, half)], second_held.at[pl.ds(0, half)], sems.at[2]),
        pltpu.make_async_copy(down_ref, second_held.at[pl.ds(half, share)], sems.at[3]),
    ]
    for copy in copies:
        copy.start()
    tall, width = first_held.shape[0] - part, first_held.shape[1]
    first_held[part:] = jnp.zeros((tall, width), BF)
    lay_beside(first_held, part, shard_ref)
    for copy in copies:
        copy.wait()
    copies = [
        pltpu.make_async_copy(first_held, first_ref, sems.at[4]),
        pltpu.make_async_copy(second_held, second_ref, sems.at[5]),
    ]
    for copy in copies:
        copy.start()
    for copy in copies:
        copy.wait()


def shards_kernel(opposite_ref, a0_ref, a1_ref, a2_ref, out_ref, held_ref, sems):
    tall, lanes = held_ref.shape[1], out_ref.shape[1]
    part = a0_ref.shape[0] - tall
    copies = [
        pltpu.make_async_copy(ref.at[pl.ds(part, tall)], held_ref.at[i], sems.at[i])
        for i, ref in enumerate((a0_ref, a1_ref, a2_ref))
    ]
    for copy in copies:
        copy.start()
    lay_beside(out_ref, 3 * tall, opposite_ref)
    for i, copy in enumerate(copies):
        copy.wait()
        out_ref[i * tall : (i + 1) * tall] = held_ref[i, :, :lanes]


def front_kernel(tall_ref, conv_ref, latent_ref, context_ref, routes_ref, out_ref, table_ref, wide_ref):
    frames, rows, cols, chans = tall_ref.shape
    tok, width = context_ref.shape
    slots = table_ref.shape[1]

    flat = tall_ref[...].reshape(frames * rows * cols, chans).astype(F32)
    column = lax.broadcasted_iota(jnp.int32, flat.shape, 0) % cols
    wide_ref[:, :chans] = jnp.where(column == 0, 0.0, pltpu.roll(flat, 1, 0)).astype(BF)
    wide_ref[:, chans : 2 * chans] = flat.astype(BF)
    wide_ref[:, 2 * chans :] = jnp.where(column == cols - 1, 0.0, pltpu.roll(flat, flat.shape[0] - 1, 0)).astype(BF)

    size = (rows - 2) * cols
    out_row = lax.broadcasted_iota(jnp.int32, (size, size), 0)
    kind, token = out_row // (size // 4), out_row % (size // 4)
    source = (token // (cols // 2) * 2 + kind // 2) * cols + token % (cols // 2) * 2 + kind % 2
    sort = (source == lax.broadcasted_iota(jnp.int32, (size, size), 1)).astype(BF)
    lat = latent_ref.shape[1] // 8
    lane = lax.broadcasted_iota(jnp.int32, latent_ref.shape, 1) // lat
    patches = jnp.zeros((tok, 8 * lat), F32)
    for frame in range(frames - 2):
        mixed = jnp.zeros((size, chans), F32)
        for a in range(3):
            for b in range(3):
                at = ((frame + a) * rows + b) * cols
                mixed += dot(wide_ref[at : at + size], conv_ref[a, b])
        video = tall_ref[frame + 2, 1 : rows - 1].reshape(size, chans).astype(F32)
        feature = (video + silu(mixed)).astype(BF)
        feature = dot(sort, feature).astype(BF)
        for part in range(4):
            weight = jnp.where(lane == frame * 4 + part, latent_ref[...], jnp.zeros((), BF))
            patches += dot(feature[part * tok : (part + 1) * tok], weight)
    patches = patches.astype(BF)

    slot = lax.broadcasted_iota(jnp.int32, (tok, slots), 1)
    chosen = (routes_ref[:, :1] == slot // 2) | (routes_ref[:, 1:] == slot // 2)
    order = [lax.broadcasted_iota(jnp.int32, (tok, tok), axis) for axis in (0, 1)]
    before = dot((order[0] > order[1]).astype(BF), chosen.astype(BF))
    table = (chosen & (before == (slot % 2).astype(F32))).astype(BF)
    table_ref[...] = table
    out_ref[:, :width] = dot(table, context_ref[...], ((0,), (0,))).astype(BF)
    out_ref[:, width:] = dot(table, patches, ((0,), (0,))).astype(BF)


def swap_kernel(rows_ref, near_ref, far_ref, out_ref):
    slots, lanes = rows_ref.shape[0], near_ref.shape[1]
    out_ref[:slots] = rows_ref[...]
    out_ref[slots:, :lanes] = near_ref[...]
    out_ref[slots:, lanes : 2 * lanes] = far_ref[...]
    out_ref[slots:, 2 * lanes :] = jnp.zeros((near_ref.shape[0], out_ref.shape[1] - 2 * lanes), BF)


def near_kernel(
    at_ref,
    mine_ref,
    theirs_ref,
    router_ref,
    a0_ref,
    b0_ref,
    a1_ref,
    b1_ref,
    a2_ref,
    b2_ref,
    tokens_ref,
    score_ref,
    total_ref,
    held_ref,
    embed_ref,
    sems,
):
    yh, x, c = at_ref[0], at_ref[1], at_ref[2]
    rows, width = tokens_ref.shape[0] // 2, total_ref.shape[1]
    part = b0_ref.shape[0]
    share = part * 2 // 3
    copies = [
        pltpu.make_async_copy(ref.at[pl.ds(0, part)], held_ref.at[i // 2, pl.ds(i % 2 * part, part)], sems.at[i])
        for i, ref in enumerate((a0_ref, b0_ref, a1_ref, b1_ref, a2_ref, b2_ref))
    ]
    for copy in copies:
        copy.start()
    tall = (mine_ref.shape[0] - rows) // 4
    tiles = embed_ref.shape[1] // tall
    for core, ref in enumerate((mine_ref, theirs_ref)):
        for i, turn in enumerate((0, 3, 1, 2)):
            for j in range(2 * tiles):
                shard = (yh ^ j // tiles) * 8 + lax.rem(x + turn, 4) * 2 + (c ^ core)
                at = rows + i * tall
                embed_ref[shard, j % tiles * tall : (j % tiles + 1) * tall] = ref[at : at + tall, j * 128 : (j + 1) * 128]
    embed = embed_ref[...].reshape(width, 128)
    router = jnp.where(yh == 0, router_ref[:1], router_ref[1:]).astype(F32)
    for half, ref in enumerate((theirs_ref, mine_ref)):
        embedded = dot(ref[:rows, width:], embed, ((1,), (1,))).astype(BF)
        total = embedded.astype(F32) + ref[:rows, :width].astype(F32)
        meansq = jnp.mean(total * total, axis=1, keepdims=True)
        tokens = (total * lax.rsqrt(meansq + 1e-06)).astype(BF)
        logit = jnp.sum(tokens.astype(F32) * router, axis=1, keepdims=True)
        at = slice(half * rows, (half + 1) * rows)
        tokens_ref[at] = tokens
        score_ref[at] = 1.0 / (1.0 + jnp.exp(-logit))
    hidden = []
    for i in range(3):
        copies[2 * i].wait()
        copies[2 * i + 1].wait()
        both = dot(tokens_ref[...], held_ref[i, : 2 * share], ((1,), (1,)))
        hidden.append((silu(both[:, :share]) * both[:, share:]).astype(BF))
    hidden = jnp.concatenate(hidden, axis=1)
    tile = 512
    for at in range(0, width, tile):
        down = jnp.concatenate([held_ref[i, 2 * share :, at : at + tile] for i in range(3)], axis=0)
        total_ref[:, at : at + tile] = dot(hidden, down)


def last_kernel(tokens_ref, score_ref, total_ref, w0_ref, w1_ref, other_ref, own_ref, held_ref, sems):
    rows, width = other_ref.shape
    part, share = w1_ref.shape[0], held_ref.shape[0] // 3
    copies = [
        pltpu.make_async_copy(ref.at[pl.ds(0, part)], held_ref.at[pl.ds(i * part, part)], sems.at[i])
        for i, ref in enumerate((w0_ref, w1_ref))
    ]
    for copy in copies:
        copy.start()
    for copy in copies:
        copy.wait()
    both = dot(tokens_ref[...], held_ref[: 2 * share], ((1,), (1,)))
    hidden = (silu(both[:, :share]) * both[:, share:]).astype(BF)
    tile = 512
    for at in range(0, width, tile):
        cut = slice(at, at + tile)
        total = total_ref[:, cut] + dot(hidden, held_ref[2 * share :, cut])
        total = (total * score_ref[...]).astype(BF)
        other_ref[:, cut] = total[:rows]
        own_ref[:, cut] = total[rows:]


def local(
    video,
    conv_weight,
    latent_weight,
    embed_weight,
    context,
    router_weight,
    gate_weight,
    up_weight,
    down_weight,
    routes,
):
    rows, cols = video.shape[1:3]
    tok, width = context.shape
    experts, capacity = 64, 2
    slots = experts * capacity
    share = down_weight.shape[1]
    hbm = pl.BlockSpec(memory_space=pltpu.HBM)
    vmem = pl.BlockSpec(memory_space=pltpu.VMEM)
    smem = pl.BlockSpec(memory_space=pltpu.SMEM)
    params = pltpu.CompilerParams(vmem_limit_bytes=VMEM_BYTES)

    past = shifted(video, FRAME, 1)
    shard = embed_weight.T
    opposite = ring(shard, 2)
    past, opposite = lax.optimization_barrier((past, opposite))
    part, tall = 3 * share // 2, 16
    first, second = pl.pallas_call(
        pack_kernel,
        out_shape=[jax.ShapeDtypeStruct((part + tall, width), BF), jax.ShapeDtypeStruct((part, width), BF)],
        in_specs=[hbm] * 3 + [vmem],
        out_specs=[hbm] * 2,
        scratch_shapes=[
            pltpu.VMEM((part + tall, width), BF),
            pltpu.VMEM((part, width), BF),
            pltpu.SemaphoreType.DMA((6,)),
        ],
        compiler_params=pltpu.CompilerParams(vmem_limit_bytes=PACK_BYTES),
    )(gate_weight[0].T, up_weight[0].T, down_weight[0], shard)
    first_behind, second_ahead = ring(first, -1), ring(second, 1)
    first_ahead, second_behind = ring(first, 1), ring(second, -1)
    first_opposite, second_opposite = ring(first_behind, -1), ring(second_ahead, 1)

    stacked = jnp.concatenate([past, video], axis=0)
    above = shifted(stacked[:, rows - 1 :], EXPERT, 1)
    below = shifted(stacked[:, :1], EXPERT, -1)
    padded = jnp.concatenate([above, stacked, below], axis=1)
    chans = video.shape[3]
    raw = width + embed_weight.shape[0]
    outgoing, table = pl.pallas_call(
        front_kernel,
        out_shape=[jax.ShapeDtypeStruct((slots, raw), BF), jax.ShapeDtypeStruct((tok, slots), BF)],
        in_specs=[vmem] * 5,
        out_specs=[vmem] * 2,
        scratch_shapes=[pltpu.VMEM((padded.size // chans, 3 * chans), BF)],
        compiler_params=params,
    )(padded, conv_weight.reshape(3, 3, 3 * chans, chans), jnp.tile(latent_weight, (1, 8)), context, routes)

    arrived = lax.all_to_all(outgoing.reshape(experts, capacity, raw), SOURCES, split_axis=0, concat_axis=0, tiled=True)
    lanes = shard.shape[0] // tall * 128
    shards = pl.pallas_call(
        shards_kernel,
        out_shape=jax.ShapeDtypeStruct((4 * tall, lanes), BF),
        in_specs=[vmem] + [hbm] * 3,
        out_specs=vmem,
        scratch_shapes=[pltpu.VMEM((3, tall, width), BF), pltpu.SemaphoreType.DMA((3,))],
        compiler_params=pltpu.CompilerParams(vmem_limit_bytes=PACK_BYTES),
    )(opposite, first, first_behind, first_ahead)
    beyond = lax.ppermute(shards, "yh", SWAP)
    arrived, beyond, second_behind = lax.optimization_barrier((arrived, beyond, second_behind))
    mine = pl.pallas_call(
        swap_kernel,
        out_shape=jax.ShapeDtypeStruct((slots + 4 * tall, raw), BF),
        in_specs=[vmem] * 3,
        out_specs=vmem,
        compiler_params=params,
    )(arrived.reshape(slots, raw), shards, beyond)
    theirs = lax.ppermute(mine, "c", SWAP)
    place = jnp.stack([lax.axis_index(axis) for axis in FRAME]).astype(jnp.int32)
    tokens, score, total = pl.pallas_call(
        near_kernel,
        out_shape=[
            jax.ShapeDtypeStruct((2 * slots, width), BF),
            jax.ShapeDtypeStruct((2 * slots, 1), F32),
            jax.ShapeDtypeStruct((2 * slots, width), F32),
        ],
        in_specs=[smem] + [vmem] * 3 + [hbm] * 6,
        out_specs=[vmem] * 3,
        scratch_shapes=[
            pltpu.VMEM((3, 3 * share, width), BF),
            pltpu.VMEM((16, embed_weight.shape[1], 128), BF),
            pltpu.SemaphoreType.DMA((6,)),
        ],
        compiler_params=params,
    )(place, mine, theirs, router_weight[:, :, 0], first, second, first_behind, second_behind, first_ahead, second_ahead)
    other, own = pl.pallas_call(
        last_kernel,
        out_shape=[jax.ShapeDtypeStruct((slots, width), BF)] * 2,
        in_specs=[vmem] * 3 + [hbm] * 2,
        out_specs=[vmem] * 2,
        scratch_shapes=[pltpu.VMEM((3 * share, width), BF), pltpu.SemaphoreType.DMA((2,))],
        compiler_params=params,
    )(tokens, score, total, first_opposite, second_opposite)
    back = lax.ppermute(other, "c", SWAP)
    summed = (back.astype(F32) + own.astype(F32)).astype(BF).reshape(experts, capacity, width)
    homeward = lax.all_to_all(summed, SOURCES, split_axis=0, concat_axis=0, tiled=True)
    return dot(table, homeward.reshape(slots, width)).astype(BF)


def solution(mesh):
    fine = Mesh(mesh.devices.reshape(SIZES), NAMES)
    return jax.shard_map(
        local,
        mesh=fine,
        in_specs=(
            P(FRAME, EXPERT, None, None),
            P(),
            P(),
            P(None, FRAME),
            P((*FRAME, *EXPERT), None),
            P(None, None, EXPERT),
            P(EXPERT, None, FRAME),
            P(EXPERT, None, FRAME),
            P(EXPERT, FRAME, None),
            P((*FRAME, *EXPERT), None),
        ),
        out_specs=P((*FRAME, *EXPERT), None),
        check_vma=False,
    )
```

```python
import jax
import jax.numpy as jnp
from jax import lax
from jax.experimental import pallas as pl
from jax.experimental.pallas import tpu as pltpu
from jax.sharding import Mesh, PartitionSpec as P

FRAME = ("yh", "x", "c")
EXPERT = ("yl", "z")
SOURCES = ("yh", "yl", "z")
SIZES = (2, 4, 2, 4, 8)
NAMES = ("yh", "x", "c", "yl", "z")
BF = jnp.bfloat16
F32 = jnp.float32
SWAP = [(0, 1), (1, 0)]
VMEM_BYTES = 16 * 1024 * 1024
PACK_BYTES = 66_400_000


def dot(a, b, dims=((1,), (0,))):
    return lax.dot_general(a, b, (dims, ((), ())), preferred_element_type=F32)


def shifted(value, axes, step):
    count = lax.axis_size(axes)
    pairs = [(i, i + step) for i in range(count) if 0 <= i + step < count]
    return lax.ppermute(value, axes, pairs)


def ring(value, step):
    return lax.ppermute(value, "x", [(i, (i - step) % 4) for i in range(4)])


def silu(value):
    return value / (1.0 + jnp.exp(-value))


def lay_beside(out_ref, at, ref, lane=0):
    tall = 16
    for i in range(ref.shape[0] // tall):
        lanes = slice(lane + i * 128, lane + (i + 1) * 128)
        out_ref[at : at + tall, lanes] = ref[i * tall : (i + 1) * tall]


def pack_kernel(gate_ref, up_ref, down_ref, shard_ref, first_ref, second_ref, first_held, second_held, sems):
    share = down_ref.shape[0]
    half, part = share // 2, 3 * share // 2
    copies = [
        pltpu.make_async_copy(gate_ref, first_held.at[pl.ds(0, share)], sems.at[0]),
        pltpu.make_async_copy(up_ref.at[pl.ds(0, half)], first_held.at[pl.ds(share, half)], sems.at[1]),
        pltpu.make_async_copy(up_ref.at[pl.ds(half, half)], second_held.at[pl.ds(0, half)], sems.at[2]),
        pltpu.make_async_copy(down_ref, second_held.at[pl.ds(half, share)], sems.at[3]),
    ]
    for copy in copies:
        copy.start()
    tall, width = first_held.shape[0] - part, first_held.shape[1]
    for ref in (first_held, second_held):
        ref[part:] = jnp.zeros((tall, width), BF)
        lay_beside(ref, part, shard_ref)
    for copy in copies:
        copy.wait()
    copies = [
        pltpu.make_async_copy(first_held, first_ref, sems.at[4]),
        pltpu.make_async_copy(second_held, second_ref, sems.at[5]),
    ]
    for copy in copies:
        copy.start()
    for copy in copies:
        copy.wait()


def shards_kernel(opposite_ref, a0_ref, a1_ref, a2_ref, out_ref, held_ref, sems):
    tall, lanes = held_ref.shape[1], out_ref.shape[1]
    part = a0_ref.shape[0] - tall
    copies = [
        pltpu.make_async_copy(ref.at[pl.ds(part, tall)], held_ref.at[i], sems.at[i])
        for i, ref in enumerate((a0_ref, a1_ref, a2_ref))
    ]
    for copy in copies:
        copy.start()
    lay_beside(out_ref, 3 * tall, opposite_ref)
    for i, copy in enumerate(copies):
        copy.wait()
        out_ref[i * tall : (i + 1) * tall] = held_ref[i, :, :lanes]


def front_kernel(tall_ref, conv_ref, latent_ref, context_ref, routes_ref, out_ref, table_ref, wide_ref):
    frames, rows, cols, chans = tall_ref.shape
    tok, width = context_ref.shape
    slots = table_ref.shape[1]

    flat = tall_ref[...].reshape(frames * rows * cols, chans).astype(F32)
    column = lax.broadcasted_iota(jnp.int32, flat.shape, 0) % cols
    wide_ref[:, :chans] = jnp.where(column == 0, 0.0, pltpu.roll(flat, 1, 0)).astype(BF)
    wide_ref[:, chans : 2 * chans] = flat.astype(BF)
    wide_ref[:, 2 * chans :] = jnp.where(column == cols - 1, 0.0, pltpu.roll(flat, flat.shape[0] - 1, 0)).astype(BF)

    size = (rows - 2) * cols
    out_row = lax.broadcasted_iota(jnp.int32, (size, size), 0)
    kind, token = out_row // (size // 4), out_row % (size // 4)
    source = (token // (cols // 2) * 2 + kind // 2) * cols + token % (cols // 2) * 2 + kind % 2
    sort = (source == lax.broadcasted_iota(jnp.int32, (size, size), 1)).astype(BF)
    lat = latent_ref.shape[1] // 8
    lane = lax.broadcasted_iota(jnp.int32, latent_ref.shape, 1) // lat
    patches = jnp.zeros((tok, 8 * lat), F32)
    for frame in range(frames - 2):
        mixed = jnp.zeros((size, chans), F32)
        for a in range(3):
            for b in range(3):
                at = ((frame + a) * rows + b) * cols
                mixed += dot(wide_ref[at : at + size], conv_ref[a, b])
        video = tall_ref[frame + 2, 1 : rows - 1].reshape(size, chans).astype(F32)
        feature = (video + silu(mixed)).astype(BF)
        feature = dot(sort, feature).astype(BF)
        for part in range(4):
            weight = jnp.where(lane == frame * 4 + part, latent_ref[...], jnp.zeros((), BF))
            patches += dot(feature[part * tok : (part + 1) * tok], weight)
    patches = patches.astype(BF)

    slot = lax.broadcasted_iota(jnp.int32, (tok, slots), 1)
    chosen = (routes_ref[:, :1] == slot // 2) | (routes_ref[:, 1:] == slot // 2)
    order = [lax.broadcasted_iota(jnp.int32, (tok, tok), axis) for axis in (0, 1)]
    before = dot((order[0] > order[1]).astype(BF), chosen.astype(BF))
    table = (chosen & (before == (slot % 2).astype(F32))).astype(BF)
    table_ref[...] = table
    out_ref[:, :width] = dot(table, context_ref[...], ((0,), (0,))).astype(BF)
    out_ref[:, width:] = dot(table, patches, ((0,), (0,))).astype(BF)


def swap_kernel(rows_ref, near_ref, far_ref, out_ref):
    slots, lanes = rows_ref.shape[0], near_ref.shape[1]
    out_ref[:slots] = rows_ref[...]
    out_ref[slots:, :lanes] = near_ref[...]
    out_ref[slots:, lanes : 2 * lanes] = far_ref[...]
    out_ref[slots:, 2 * lanes :] = jnp.zeros((near_ref.shape[0], out_ref.shape[1] - 2 * lanes), BF)


def near_kernel(
    at_ref,
    mine_ref,
    theirs_ref,
    router_ref,
    a0_ref,
    b0_ref,
    a1_ref,
    b1_ref,
    a2_ref,
    b2_ref,
    tokens_ref,
    score_ref,
    total_ref,
    held_ref,
    embed_ref,
    sems,
):
    yh, x, c = at_ref[0], at_ref[1], at_ref[2]
    rows, width = tokens_ref.shape[0] // 2, total_ref.shape[1]
    part, share = held_ref.shape[1] // 2, held_ref.shape[1] // 3
    copies = [
        pltpu.make_async_copy(ref.at[pl.ds(0, part)], held_ref.at[i // 2, pl.ds(i % 2 * part, part)], sems.at[i])
        for i, ref in enumerate((a0_ref, b0_ref, a1_ref, b1_ref, a2_ref, b2_ref))
    ]
    for copy in copies:
        copy.start()
    tall = (mine_ref.shape[0] - rows) // 4
    tiles = embed_ref.shape[1] // tall
    for core, ref in enumerate((mine_ref, theirs_ref)):
        for i, turn in enumerate((0, 3, 1, 2)):
            for j in range(2 * tiles):
                shard = (yh ^ j // tiles) * 8 + lax.rem(x + turn, 4) * 2 + (c ^ core)
                at = rows + i * tall
                embed_ref[shard, j % tiles * tall : (j % tiles + 1) * tall] = ref[at : at + tall, j * 128 : (j + 1) * 128]
    embed = embed_ref[...].reshape(width, 128)
    router = jnp.where(yh == 0, router_ref[:1], router_ref[1:]).astype(F32)
    for half, ref in enumerate((theirs_ref, mine_ref)):
        embedded = dot(ref[:rows, width:], embed, ((1,), (1,))).astype(BF)
        total = embedded.astype(F32) + ref[:rows, :width].astype(F32)
        meansq = jnp.mean(total * total, axis=1, keepdims=True)
        tokens = (total * lax.rsqrt(meansq + 1e-06)).astype(BF)
        logit = jnp.sum(tokens.astype(F32) * router, axis=1, keepdims=True)
        at = slice(half * rows, (half + 1) * rows)
        tokens_ref[at] = tokens
        score_ref[at] = 1.0 / (1.0 + jnp.exp(-logit))
    hidden = []
    for i in range(3):
        copies[2 * i].wait()
        copies[2 * i + 1].wait()
        both = dot(tokens_ref[...], held_ref[i, : 2 * share], ((1,), (1,)))
        hidden.append((silu(both[:, :share]) * both[:, share:]).astype(BF))
    hidden = jnp.concatenate(hidden, axis=1)
    tile = 512
    for at in range(0, width, tile):
        down = jnp.concatenate([held_ref[i, 2 * share :, at : at + tile] for i in range(3)], axis=0)
        total_ref[:, at : at + tile] = dot(hidden, down)


def last_kernel(tokens_ref, score_ref, total_ref, w0_ref, w1_ref, other_ref, own_ref, held_ref, sems):
    rows, width = other_ref.shape
    part, share = held_ref.shape[0] // 2, held_ref.shape[0] // 3
    copies = [
        pltpu.make_async_copy(ref.at[pl.ds(0, part)], held_ref.at[pl.ds(i * part, part)], sems.at[i])
        for i, ref in enumerate((w0_ref, w1_ref))
    ]
    for copy in copies:
        copy.start()
    for copy in copies:
        copy.wait()
    both = dot(tokens_ref[...], held_ref[: 2 * share], ((1,), (1,)))
    hidden = (silu(both[:, :share]) * both[:, share:]).astype(BF)
    tile = 512
    for at in range(0, width, tile):
        cut = slice(at, at + tile)
        total = total_ref[:, cut] + dot(hidden, held_ref[2 * share :, cut])
        total = (total * score_ref[...]).astype(BF)
        other_ref[:, cut] = total[:rows]
        own_ref[:, cut] = total[rows:]


def local(
    video,
    conv_weight,
    latent_weight,
    embed_weight,
    context,
    router_weight,
    gate_weight,
    up_weight,
    down_weight,
    routes,
):
    rows, cols = video.shape[1:3]
    tok, width = context.shape
    experts, capacity = 64, 2
    slots = experts * capacity
    share = down_weight.shape[1]
    hbm = pl.BlockSpec(memory_space=pltpu.HBM)
    vmem = pl.BlockSpec(memory_space=pltpu.VMEM)
    smem = pl.BlockSpec(memory_space=pltpu.SMEM)
    params = pltpu.CompilerParams(vmem_limit_bytes=VMEM_BYTES)

    past = shifted(video, FRAME, 1)
    shard = embed_weight.T
    opposite = ring(shard, 2)
    past, opposite = lax.optimization_barrier((past, opposite))
    part, tall = 3 * share // 2, 16
    first, second = pl.pallas_call(
        pack_kernel,
        out_shape=[jax.ShapeDtypeStruct((part + tall, width), BF)] * 2,
        in_specs=[hbm] * 3 + [vmem],
        out_specs=[hbm] * 2,
        scratch_shapes=[pltpu.VMEM((part + tall, width), BF)] * 2 + [pltpu.SemaphoreType.DMA((6,))],
        compiler_params=pltpu.CompilerParams(vmem_limit_bytes=PACK_BYTES),
    )(gate_weight[0].T, up_weight[0].T, down_weight[0], shard)
    first_behind, second_ahead = ring(first, -1), ring(second, 1)
    first_ahead, second_behind = ring(first, 1), ring(second, -1)
    first_opposite, second_opposite = ring(first_behind, -1), ring(second_ahead, 1)

    stacked = jnp.concatenate([past, video], axis=0)
    above = shifted(stacked[:, rows - 1 :], EXPERT, 1)
    below = shifted(stacked[:, :1], EXPERT, -1)
    padded = jnp.concatenate([above, stacked, below], axis=1)
    chans = video.shape[3]
    raw = width + embed_weight.shape[0]
    outgoing, table = pl.pallas_call(
        front_kernel,
        out_shape=[jax.ShapeDtypeStruct((slots, raw), BF), jax.ShapeDtypeStruct((tok, slots), BF)],
        in_specs=[vmem] * 5,
        out_specs=[vmem] * 2,
        scratch_shapes=[pltpu.VMEM((padded.size // chans, 3 * chans), BF)],
        compiler_params=params,
    )(padded, conv_weight.reshape(3, 3, 3 * chans, chans), jnp.tile(latent_weight, (1, 8)), context, routes)

    arrived = lax.all_to_all(outgoing.reshape(experts, capacity, raw), SOURCES, split_axis=0, concat_axis=0, tiled=True)
    lanes = shard.shape[0] // tall * 128
    shards = pl.pallas_call(
        shards_kernel,
        out_shape=jax.ShapeDtypeStruct((4 * tall, lanes), BF),
        in_specs=[vmem] + [hbm] * 3,
        out_specs=vmem,
        scratch_shapes=[pltpu.VMEM((3, tall, width), BF), pltpu.SemaphoreType.DMA((3,))],
        compiler_params=pltpu.CompilerParams(vmem_limit_bytes=PACK_BYTES),
    )(opposite, first, first_behind, second_ahead)
    beyond = lax.ppermute(shards, "yh", SWAP)
    arrived, beyond, first_ahead, second_behind = lax.optimization_barrier(
        (arrived, beyond, first_ahead, second_behind)
    )
    mine = pl.pallas_call(
        swap_kernel,
        out_shape=jax.ShapeDtypeStruct((slots + 4 * tall, raw), BF),
        in_specs=[vmem] * 3,
        out_specs=vmem,
        compiler_params=params,
    )(arrived.reshape(slots, raw), shards, beyond)
    theirs = lax.ppermute(mine, "c", SWAP)
    place = jnp.stack([lax.axis_index(axis) for axis in FRAME]).astype(jnp.int32)
    tokens, score, total = pl.pallas_call(
        near_kernel,
        out_shape=[
            jax.ShapeDtypeStruct((2 * slots, width), BF),
            jax.ShapeDtypeStruct((2 * slots, 1), F32),
            jax.ShapeDtypeStruct((2 * slots, width), F32),
        ],
        in_specs=[smem] + [vmem] * 3 + [hbm] * 6,
        out_specs=[vmem] * 3,
        scratch_shapes=[
            pltpu.VMEM((3, 3 * share, width), BF),
            pltpu.VMEM((16, embed_weight.shape[1], 128), BF),
            pltpu.SemaphoreType.DMA((6,)),
        ],
        compiler_params=params,
    )(place, mine, theirs, router_weight[:, :, 0], first, second, first_behind, second_behind, first_ahead, second_ahead)
    other, own = pl.pallas_call(
        last_kernel,
        out_shape=[jax.ShapeDtypeStruct((slots, width), BF)] * 2,
        in_specs=[vmem] * 3 + [hbm] * 2,
        out_specs=[vmem] * 2,
        scratch_shapes=[pltpu.VMEM((3 * share, width), BF), pltpu.SemaphoreType.DMA((2,))],
        compiler_params=params,
    )(tokens, score, total, first_opposite, second_opposite)
    back = lax.ppermute(other, "c", SWAP)
    summed = (back.astype(F32) + own.astype(F32)).astype(BF).reshape(experts, capacity, width)
    homeward = lax.all_to_all(summed, SOURCES, split_axis=0, concat_axis=0, tiled=True)
    return dot(table, homeward.reshape(slots, width)).astype(BF)


def solution(mesh):
    fine = Mesh(mesh.devices.reshape(SIZES), NAMES)
    return jax.shard_map(
        local,
        mesh=fine,
        in_specs=(
            P(FRAME, EXPERT, None, None),
            P(),
            P(),
            P(None, FRAME),
            P((*FRAME, *EXPERT), None),
            P(None, None, EXPERT),
            P(EXPERT, None, FRAME),
            P(EXPERT, None, FRAME),
            P(EXPERT, FRAME, None),
            P((*FRAME, *EXPERT), None),
        ),
        out_specs=P((*FRAME, *EXPERT), None),
        check_vma=False,
    )
```
